128 devices in a mesh: seq: 16 (over y_hi, z, core), tp: 8 (over y_lo, x).
Axes of the slice: x: 4, y: 4 (y_hi: 2, y_lo: 2; y = y_hi * 2 + y_lo), z: 4, core: 2. Of those that a mesh axis runs over, the one named last changes fastest.
Arguments:
- queries: bfloat16 [8192, 4096], P('seq', 'tp'), may hold values from -6 to 6
- keys: bfloat16 [8192, 4096], P('seq', 'tp'), may hold values from -6 to 6
- values: bfloat16 [8192, 4096], P('seq', 'tp'), may hold values from -16 to 16
- offsets: int32 [3, 32], replicated, may hold values from 0 to 7, as said below
- out_weight: bfloat16 [4096, 4096], P('tp'), may hold values from -0.09375 to 0.09375
- out_grad: bfloat16 [8192, 4096], P('seq', 'tp'), may hold values from -6 to 6
Outputs:
- result: bfloat16 [8192, 4096], P('seq', 'tp')
- grad_queries: bfloat16 [8192, 4096], P('seq', 'tp')
- grad_keys: bfloat16 [8192, 4096], P('seq', 'tp')
- grad_values: bfloat16 [8192, 4096], P('seq', 'tp')
- grad_weight: bfloat16 [4096, 4096], P('tp', 'seq')
The draws below stay inside these ranges and needn't reach their ends.
Inputs may be any that keep to these rules, and one draw needn't show every extreme that they name: offsets[j, h] is below 2^(j+1).
All inputs are finite; a program needn't handle non-finite values.
Results may differ from the reference program's by a relative error of at most 0.023.
Values may be sent and summed in bfloat16 or wider, within the bound.
A program may use at most 128 MiB of HBM per device.

```python
import jax
import jax.numpy as jnp
from jax import lax

D = 4096
H = 32
DH = 128
SEG = 512
LEV = 3
TOKENS = 8192
N_SEQ = 16


def draw_queries(key, part):
    key = jax.random.fold_in(key, 1)
    return jnp.clip(jax.random.normal(key, (TOKENS, D)), -6.0, 6.0).astype(jnp.bfloat16)


def draw_keys(key, part):
    key = jax.random.fold_in(key, 2)
    return jnp.clip(jax.random.normal(key, (TOKENS, D)), -6.0, 6.0).astype(jnp.bfloat16)


def draw_offsets(key, part):
    key = jax.random.fold_in(key, 3)
    dilations = 2 ** jnp.arange(1, LEV + 1, dtype=jnp.int32)
    raw = jax.random.randint(key, (LEV, H), 0, 1 << 30)
    phases = raw % dilations[:, None]
    top_head = jax.random.randint(jax.random.fold_in(key, 5), (), 0, H)
    low_head = jax.random.randint(jax.random.fold_in(key, 6), (), 0, H)
    phases = phases.at[LEV - 1, top_head].set(2 ** LEV - 1)
    phases = phases.at[0, low_head].set(0)
    return phases.astype(jnp.int32)


def spiked(values, rng, source, target, blocks, factor):
    def block_of(position):
        return (jnp.arange(values.shape[position]) // (values.shape[position] // blocks)).reshape((-1,) + (1,) * (values.ndim - 1 - position))

    first = jax.random.permutation(rng, blocks)[block_of(target)]
    second = (block_of(target) + blocks // 2) % blocks
    return jnp.where((block_of(source) == first) | (block_of(source) == second), factor * values, values)


def shard_levels(stream_key, shape, pieces, low, high):
    gain = 1.0
    for axis_at, blocks in pieces:
        draws = jax.random.uniform(jax.random.fold_in(jax.random.fold_in(stream_key, 6), axis_at), (blocks,), jnp.float32, low / len(pieces), high / len(pieces))
        gain = gain * jnp.repeat(jnp.exp(draws), shape[axis_at] // blocks).reshape((-1,) + (1,) * (len(shape) - 1 - axis_at))
    return gain


def noise(stream_key, dims, spread, bound, shards=(), held_as=jnp.bfloat16):
    drawn = jax.random.normal(stream_key, dims, jnp.float32) * spread
    if len(shards) > 0:
        drawn = shard_levels(stream_key, dims, shards, -0.22, 0.18) * drawn
    return jnp.clip(drawn, min=-bound, max=bound).astype(held_as)


def gaussian_with(key, dims, deviation, limit, cuts, heavy, kind=jnp.bfloat16):
    array = deviation * jax.random.normal(key, dims, jnp.float32)
    if cuts:
        array = array * shard_levels(key, dims, cuts, -0.22, 0.18)
    return jnp.clip(spiked(array, jax.random.fold_in(key, 3), *heavy), -limit, limit).astype(kind)


def setup_inputs(seed: int = 0) -> dict:
    key_of = jax.random.split(jax.random.key(seed), 7)
    return {
        "queries": draw_queries(jax.random.fold_in(key_of[6], 71), 0),
        "keys": draw_keys(jax.random.fold_in(key_of[6], 71), 0),
        "values": noise(key_of[2], (TOKENS, D), 3.0, 16.0, ((0, 16), (1, 8))),
        "offsets": draw_offsets(jax.random.fold_in(key_of[6], 71), 0),
        "out_weight": noise(key_of[4], (D, D), D ** -0.5, 0.09375, ((0, 8),)),
        "out_grad": gaussian_with(key_of[5], (TOKENS, D), 1.0, 6.0, ((0, 16), (1, 8)), (0, 1, 16, 2.0)),
    }


def widened(source):
    return lax.optimization_barrier(source.astype(jnp.bfloat16)).astype(jnp.float32)


def select_rows(source, width, dilation, chosen_mask):
    segments = source.shape[0] // width
    shaped = source.reshape((segments, width // dilation, dilation) + source.shape[1:])
    selector = chosen_mask.reshape(chosen_mask.shape + (1,) * (source.ndim - 2))
    return jnp.sum(jnp.where(selector, shaped, jnp.zeros((), source.dtype)), axis=2)


def spread_rows(source, chosen_mask):
    selector = chosen_mask.reshape(chosen_mask.shape + (1,) * (source.ndim - 3))
    spread_out = jnp.where(selector, source[:, :, None], jnp.zeros((), source.dtype))
    return spread_out.reshape((-1,) + source.shape[2:])


def level_forward(query_part, key_part, value_part):
    score_scale = DH ** -0.5

    def one_segment(parts):
        query_seg, key_seg, value_seg = parts
        scores = jnp.einsum("qhe,khe->hqk", query_seg.astype(jnp.float32), key_seg.astype(jnp.float32)) * score_scale
        row_max = jnp.max(scores, axis=2)
        exp_scores = jnp.exp(scores - row_max[..., None])
        row_sum = jnp.sum(exp_scores, axis=2)
        weighted = jnp.einsum("hqk,khe->qhe", widened(exp_scores), value_seg.astype(jnp.float32))
        return row_max.T, row_sum.T, weighted

    return lax.map(one_segment, (query_part, key_part, value_part))


def level_backward(query_part, key_part, value_part, grad_part, lse_part, delta_part):
    score_scale = DH ** -0.5

    def one_segment(parts):
        query_seg, key_seg, value_seg, grad_seg, lse_seg, delta_seg = parts
        query_wide = query_seg.astype(jnp.float32)
        key_wide = key_seg.astype(jnp.float32)
        grad_wide = grad_seg.astype(jnp.float32)
        scores = jnp.einsum("qhe,khe->hqk", query_wide, key_wide) * score_scale
        probs = jnp.exp(scores - lse_seg.T[..., None])
        grad_v = jnp.einsum("hqk,qhe->khe", widened(probs), grad_wide)
        grad_p = jnp.einsum("qhe,khe->hqk", grad_wide, value_seg.astype(jnp.float32))
        grad_s = widened(probs * (grad_p - delta_seg.T[..., None]))
        grad_q = jnp.einsum("hqk,khe->qhe", grad_s, key_wide) * score_scale
        grad_k = jnp.einsum("hqk,qhe->khe", grad_s, query_wide) * score_scale
        return grad_q, grad_k, grad_v

    return lax.map(one_segment, (query_part, key_part, value_part, grad_part, lse_part, delta_part))


def reference(queries, keys, values, offsets, out_weight, out_grad):
    query_all = queries.reshape(TOKENS, H, DH)
    key_all = keys.reshape(TOKENS, H, DH)
    value_all = values.reshape(TOKENS, H, DH)
    level_specs = [(SEG, 1, jnp.ones((1, H), dtype=bool))]
    for level_number in range(1, LEV + 1):
        dilation = 2 ** level_number
        chosen_mask = jnp.arange(dilation, dtype=jnp.int32)[:, None] == offsets[level_number - 1][None, :]
        level_specs.append((SEG * dilation, dilation, chosen_mask))
    partials = []
    for width, dilation, chosen_mask in level_specs:
        part_max, part_sum, part_weighted = level_forward(
            select_rows(query_all, width, dilation, chosen_mask),
            select_rows(key_all, width, dilation, chosen_mask),
            select_rows(value_all, width, dilation, chosen_mask))
        covered = jnp.broadcast_to(chosen_mask[None, None], (TOKENS // width, width // dilation, dilation, H)).reshape(TOKENS, H)
        partials.append((covered, spread_rows(part_max, chosen_mask), spread_rows(part_sum, chosen_mask), spread_rows(part_weighted, chosen_mask)))
    base_max = partials[0][1]
    overall = base_max
    for entry in partials[1:]:
        overall = jnp.maximum(overall, jnp.where(entry[0], entry[1], base_max))
    softmax_total = jnp.zeros((TOKENS, H), jnp.float32)
    accumulated = jnp.zeros((TOKENS, H, DH), jnp.float32)
    for entry in partials:
        level_factor = jnp.where(entry[0], jnp.exp(jnp.where(entry[0], entry[1], overall) - overall), 0.0)
        softmax_total = softmax_total + level_factor * entry[2]
        accumulated = accumulated + level_factor[..., None] * entry[3]
    attended = (accumulated / softmax_total[..., None]).astype(jnp.bfloat16)
    log_total = overall + jnp.log(softmax_total)
    attended_flat = attended.reshape(TOKENS, D)
    result = jnp.dot(attended_flat, out_weight, preferred_element_type=jnp.float32).astype(jnp.bfloat16)
    grad_attended = jnp.dot(out_grad, out_weight.T, preferred_element_type=jnp.float32).astype(jnp.bfloat16)

    def add_block(running, pair):
        term = jnp.dot(pair[0].T, pair[1], preferred_element_type=jnp.float32)
        return running + widened(term), None

    weight_total, _ = lax.scan(add_block, jnp.zeros((D, D), jnp.float32),
                               (attended_flat.reshape(N_SEQ, SEG, D), out_grad.reshape(N_SEQ, SEG, D)))
    grad_weight = weight_total.astype(jnp.bfloat16)
    grad_all = grad_attended.reshape(TOKENS, H, DH)
    delta = jnp.sum(grad_all.astype(jnp.float32) * attended.astype(jnp.float32), axis=2)
    grad_query = jnp.zeros((TOKENS, H, DH), jnp.float32)
    grad_key = jnp.zeros((TOKENS, H, DH), jnp.float32)
    grad_value = jnp.zeros((TOKENS, H, DH), jnp.float32)
    for width, dilation, chosen_mask in level_specs:
        part_q, part_k, part_v = level_backward(
            select_rows(query_all, width, dilation, chosen_mask),
            select_rows(key_all, width, dilation, chosen_mask),
            select_rows(value_all, width, dilation, chosen_mask),
            select_rows(grad_all, width, dilation, chosen_mask),
            select_rows(log_total, width, dilation, chosen_mask),
            select_rows(delta, width, dilation, chosen_mask))
        grad_query = grad_query + spread_rows(part_q, chosen_mask)
        grad_key = grad_key + spread_rows(part_k, chosen_mask)
        grad_value = grad_value + spread_rows(part_v, chosen_mask)
    return (result,
            grad_query.astype(jnp.bfloat16).reshape(TOKENS, D),
            grad_key.astype(jnp.bfloat16).reshape(TOKENS, D),
            grad_value.astype(jnp.bfloat16).reshape(TOKENS, D),
            grad_weight)
```

```python
import jax
import jax.numpy as jnp
from jax import lax
from jax.experimental import pallas as pl
from jax.experimental.pallas import tpu as pltpu
from jax.sharding import PartitionSpec as P

DH = 128
LEV = 3
R = 512
C = 512
HL = 4
SCALE = DH**-0.5
K2E = SCALE * 1.4426950408889634
NEG = -1e30
BF = jnp.bfloat16
F32 = jnp.float32

NAMES = (
    ["og1", "og3", "ogA", "ogB", "w", "wf"]
    + ["kvo1", "kvo2", "kvo3", "kv2", "kvf2"]
    + ["kv3_1", "kv3_2", "kv3_3", "kvf3_1", "kvf3_2", "kvf3_3"]
    + ["att0", "att1", "att2", "att3", "g"]
    + ["ra", "rb", "r1", "r3"]
    + ["gc0", "gc1", "gc2", "gc3", "za", "zb", "z1", "z3", "y0", "y1"]
    + ["b1_1", "b2_1", "b2_2", "b2_3"]
    + ["b3_%d" % m for m in range(1, 8)]
)
ID = {name: i for i, name in enumerate(NAMES)}


def dot(a, b):
    return lax.dot_general(a, b, (((1,), (0,)), ((), ())), preferred_element_type=F32)


def dot_t(a, b):
    return lax.dot_general(a, b, (((1,), (1,)), ((), ())), preferred_element_type=F32)


def loop(count, body):
    def step(i, carry):
        body(i)
        return carry

    lax.fori_loop(0, count, step, 0)


def kernel(
    offs, q_hbm, k_hbm, v_hbm, w_hbm, og_hbm,
    res_o, dq_o, dk_o, dv_o, gw_o,
    stage, perm, unperm, eye, qp, kp, vp, kv1, kv2, kv3, e0, e1, e2, e3, mm0, mm1, mm2, mm3,
    m_run, l_run, n_run, attp, att_buf, att_t, og_buf, wblk, g_own, g_send, g_recv, gp,
    res_s, res_a, res_b, res_r, res_own, gc_s, gc_r, gz_s, gz_a, gz_b, gz_r, gz_own, gy_s, gy_r,
    dqa, dk0, dv0, snd1, snd2, snd3, rcv1, rcv2, rcv3, back,
    ss, rs, ls,
):
    s = lax.axis_index("seq")
    t = lax.axis_index("tp")
    core = s % 2
    z = (s // 2) % 4
    yh = s // 8
    x = t % 4
    q = t // 4
    y = 2 * yh + q
    s_base = yh * 8
    s8 = s % 8
    kv = [None, kv1, kv2, kv3]
    es = [e0, e1, e2, e3]
    mms = [mm0, mm1, mm2, mm3]
    snd = [None, snd1, snd2, snd3]
    rcv = [None, rcv1, rcv2, rcv3]
    sent = []

    def to_seq(mask):
        return (s_base + (s8 ^ mask), t)

    def to_x(mask):
        return (s, q * 4 + (x ^ mask))

    def to_y(yy):
        return ((yy // 2) * 8 + s8, (yy % 2) * 4 + x)

    def remote(src, dst, name, device, extra=0):
        i = ID[name] + extra
        return pltpu.make_async_remote_copy(
            src_ref=src, dst_ref=dst, send_sem=ss.at[i], recv_sem=rs.at[i],
            device_id=device, device_id_type=pl.DeviceIdType.MESH,
        )

    def send(src, dst, name, device):
        copy = remote(src, dst, name, device)
        copy.start()
        sent.append(copy)

    def arrived(dst, name):
        remote(dst, dst, name, to_seq(1)).wait_recv()

    def head_cols(h):
        return pl.ds(pl.multiple_of(h * DH, DH), DH)

    def local(src, dst, i):
        copy = pltpu.make_async_copy(src, dst, ls.at[i])
        copy.start()
        return copy

    k_in = local(k_hbm, stage.at[0], 0)
    v_in = local(v_hbm, stage.at[1], 1)
    q_in = local(q_hbm, stage.at[2], 2)
    og_in = local(og_hbm, og_buf.at[x], 3)
    half = pl.ds(pl.multiple_of(q * 2048, 2048), 2048)
    w_in = local(w_hbm.at[:, half], wblk.at[q], 4)

    barrier = pltpu.get_barrier_semaphore()
    peers = [to_seq(m) for m in range(1, 8)] + [to_x(1), to_x(3)] + [to_y((y + d) % 4) for d in (1, 2, 3)]
    for peer in peers:
        pl.semaphore_signal(barrier, inc=1, device_id=peer, device_id_type=pl.DeviceIdType.MESH)
    pl.semaphore_wait(barrier, len(peers))

    send(og_hbm, og_buf.at[x], "og1", to_x(1))
    send(og_hbm, og_buf.at[x], "og3", to_x(3))
    w_there = pl.ds(pl.multiple_of((1 - q) * 2048 + core * 1024, 1024), 1024)
    w_mine = pl.ds(pl.multiple_of(core * 1024, 1024), 1024)
    w_other = pl.ds(pl.multiple_of((1 - core) * 1024, 1024), 1024)
    send(w_hbm.at[:, w_there], wblk.at[q, :, w_mine], "w", to_y((y + 3 + 2 * core) % 4))

    def place_of(i):
        return ((i & 1) << 8) | (((i >> 1) & 1) << 7) | (((i >> 2) & 1) << 6) | (i >> 3)

    rows_i = lax.broadcasted_iota(jnp.int32, (R, R), 0)
    cols_i = lax.broadcasted_iota(jnp.int32, (R, R), 1)
    perm[...] = jnp.where(rows_i == place_of(cols_i), 1.0, 0.0).astype(BF)
    unperm[...] = jnp.where(cols_i == place_of(rows_i), 1.0, 0.0).astype(BF)
    eye[...] = jnp.where(rows_i == cols_i, 1.0, 0.0).astype(BF)

    def permuted(src, dst):
        def tile(b):
            rows = pl.ds(pl.multiple_of(b * 256, 256), 256)
            moved = dot(perm[rows, :], src[...]).astype(BF)
            for h in range(HL):
                dst[h, rows, :] = moved[:, h * DH : (h + 1) * DH]

        loop(2, tile)

    def phase_of(level, h):
        return offs[level - 1, t * HL + h]

    def chosen(value, level, h):
        for bit in range(level):
            n = value.shape[0] // 2
            flag = jnp.full((n, DH), (phase_of(level, h) >> bit) & 1, jnp.int32)
            value = jnp.where(flag == 1, value[n:], value[:n])
        return value

    def chosen_bf(value, level, h):
        return value if level == 0 else chosen(value.astype(F32), level, h).astype(BF)

    k_in.wait()
    permuted(stage.at[0], kp)
    v_in.wait()
    permuted(stage.at[1], vp)
    for level in (3, 2, 1):
        n = R >> level
        slot = s % (1 << level)

        def fill(h, level=level, n=n, slot=slot):
            kv[level][slot, :, head_cols(h)] = chosen_bf(kp[h], level, h)
            kv[level][slot, :, head_cols(h + HL)] = chosen_bf(vp[h], level, h)

        loop(HL, fill)
        mine = kv[level].at[slot]
        if level == 3:
            for m in (2, 1, 3):
                send(mine, mine, "kv3_%d" % m, to_seq(2 * m))
        if level == 2:
            send(mine, mine, "kv2", to_seq(2))
        send(mine, mine, "kvo%d" % level, to_seq(1))
    q_in.wait()
    permuted(stage.at[2], qp)

    def placed(value, level, h, fill):
        phase = jnp.full(value.shape, phase_of(level, h), jnp.int32)
        order = [sum(((p >> (level - 1 - bit)) & 1) << bit for bit in range(level)) for p in range(1 << level)]
        return jnp.concatenate([jnp.where(phase == p, value, fill) for p in order], axis=0)

    def keys_of(level, h, which):
        if level == 0:
            return (kp, vp)[which][h]
        return kv[level][:, :, head_cols(h + HL * which)].reshape(R, DH)

    def forward(level, h):
        n = R >> level
        rows = min(n, 256)
        keys = keys_of(level, h, 0)
        vals = jnp.concatenate([keys_of(level, h, 1), jnp.ones((R, DH), BF)], axis=1)
        for b in range(0, n, rows):
            if level == 0:
                queries = qp[h, b : b + rows, :]
            else:
                queries = chosen_bf(qp[h], level, h)
            scores = dot_t(queries, keys) * K2E
            top = jnp.max(scores, axis=1, keepdims=True)
            e = jnp.exp2(scores - top).astype(BF)
            es[level][h, b : b + rows, :] = e
            nl = dot(e, vals)
            top = jnp.broadcast_to(top, (rows, DH))
            mms[level][h, b : b + rows, :] = top
            if level == 0:
                m_run[h, b : b + rows, :] = top
                n_run[h, b : b + rows, :] = nl[:, :DH]
                l_run[h, b : b + rows, :] = nl[:, DH:]
        if level > 0:
            old = m_run[h]
            this = placed(top, level, h, NEG)
            new = jnp.maximum(old, this)
            a_old = jnp.exp2(old - new)
            a_this = jnp.exp2(this - new)
            m_run[h] = new
            n_run[h] = n_run[h] * a_old + a_this * jnp.concatenate([nl[:, :DH]] * (1 << level), axis=0)
            l_run[h] = l_run[h] * a_old + a_this * jnp.concatenate([nl[:, DH:]] * (1 << level), axis=0)

    loop(HL, lambda h: forward(0, h))

    s4 = s % 4
    there = kv2.at[s4 ^ 2]
    arrived(there, "kv2")
    send(there, there, "kvf2", to_seq(1))
    arrived(kv1.at[core ^ 1], "kvo1")
    loop(HL, lambda h: forward(1, h))
    for m in (1, 3, 2):
        there = kv3.at[s8 ^ (2 * m)]
        arrived(there, "kv3_%d" % m)
        send(there, there, "kvf3_%d" % m, to_seq(1))
    arrived(kv2.at[s4 ^ 1], "kvo2")
    arrived(kv2.at[s4 ^ 3], "kvf2")
    loop(HL, lambda h: forward(2, h))

    arrived(og_buf.at[x ^ 1], "og1")
    send(og_buf.at[x ^ 1, 0:256], og_buf.at[x ^ 1, 0:256], "ogA", to_x(3))
    arrived(og_buf.at[x ^ 3], "og3")
    send(og_buf.at[x ^ 3, 256:512], og_buf.at[x ^ 3, 256:512], "ogB", to_x(1))
    w_got = wblk.at[1 - q, :, w_mine]
    arrived(w_got, "w")
    send(w_got, w_got, "wf", to_seq(1))

    arrived(kv3.at[s8 ^ 1], "kvo3")
    for m in (1, 3, 2):
        arrived(kv3.at[s8 ^ (2 * m + 1)], "kvf3_%d" % m)

    def last_level(h):
        forward(3, h)
        inverse = 1.0 / l_run[h]
        l_run[h] = inverse
        attended = (n_run[h] * inverse).astype(BF)
        attp[h] = attended
        att_buf[q, :, head_cols(h)] = dot(unperm[...], attended).astype(BF)
        block = att_buf.at[q, :, head_cols(h)]
        remote(block, block, "att0", to_y(y ^ 1), extra=h).start()

    loop(HL, last_level)
    for h in range(HL):
        block = att_buf.at[q, :, h * DH : (h + 1) * DH]
        sent.append(remote(block, block, "att%d" % h, to_y(y ^ 1)))

    og_in.wait()
    w_in.wait()
    arrived(og_buf.at[x ^ 2, 0:256], "ogA")
    arrived(og_buf.at[x ^ 2, 256:512], "ogB")
    arrived(wblk.at[1 - q, :, w_other], "wf")

    def grad_part(which, dst):
        def tile(b):
            rows = pl.ds(pl.multiple_of(b * 256, 256), 256)
            total = dot_t(og_buf[0, rows, :], wblk[which, :, 0:512])
            for xx in range(1, 4):
                total += dot_t(og_buf[xx, rows, :], wblk[which, :, xx * 512 : (xx + 1) * 512])
            dst[rows, :] = total.astype(dst.dtype)

        loop(2, tile)

    grad_part(1 - q, g_send)
    send(g_send, g_recv, "g", to_y(y ^ 1))
    grad_part(q, g_own)

    for h in range(HL):
        arrived(att_buf.at[1 - q, :, h * DH : (h + 1) * DH], "att%d" % h)
    for qq in range(2):
        for h in range(HL):
            cols = slice(h * DH, (h + 1) * DH)
            att_t[qq * 512 + h * DH : qq * 512 + (h + 1) * DH, :] = dot_t(eye[:DH, :DH], att_buf[qq, :, cols]).astype(BF)

    def weight_part(zz, cc, put):
        cols = pl.ds(pl.multiple_of(cc * 256, 256), 256)

        def tile(b):
            rows = pl.ds(pl.multiple_of(b * 256, 256), 256)
            put(rows, dot(att_t[rows, :], og_buf[zz, :, cols]))

        loop(4, tile)

    def result_part(xx, put):
        cols = pl.ds(pl.multiple_of(xx * 512, 512), 512)
        for b in range(2):
            rows = slice(b * 256, (b + 1) * 256)
            put(b, rows, dot(att_buf[0, rows, :], wblk[0, :, cols]) + dot(att_buf[1, rows, :], wblk[1, :, cols]))

    for m in (2, 3, 1, 0):

        def put_core(rows, value, m=m):
            gc_s[m, rows, :] = value.astype(BF)

        weight_part(z ^ m, 1 - core, put_core)
        send(gc_s.at[m], gc_r.at[m], "gc%d" % m, to_seq(1))

    def put_two(b, rows, value):
        res_s[0, rows, :] = value.astype(BF)

    result_part(x ^ 2, put_two)
    send(res_s.at[0, 0:256], res_a, "ra", to_x(1))
    send(res_s.at[0, 256:512], res_b, "rb", to_x(3))

    arrived(gc_r.at[2], "gc2")

    def put_z2(rows, value):
        gz_s[0, rows, :] = (value + gc_r[2, rows, :].astype(F32)).astype(BF)

    weight_part(z ^ 2, core, put_z2)
    send(gz_s.at[0, 0:512], gz_a, "za", to_seq(2))
    send(gz_s.at[0, 512:1024], gz_b, "zb", to_seq(6))

    arrived(res_a, "ra")

    def put_three(b, rows, value):
        if b == 0:
            value = value + res_a[...].astype(F32)
        res_s[1, rows, :] = value.astype(BF)

    result_part(x ^ 3, put_three)
    send(res_s.at[1], res_r.at[1], "r3", to_x(3))
    arrived(res_b, "rb")

    def put_one(b, rows, value):
        if b == 1:
            value = value + res_b[...].astype(F32)
        res_s[2, rows, :] = value.astype(BF)

    result_part(x ^ 1, put_one)
    send(res_s.at[2], res_r.at[0], "r1", to_x(1))

    def put_own(b, rows, value):
        res_own[rows, :] = value

    result_part(x, put_own)

    for m in (3, 1, 0):
        arrived(gc_r.at[m], "gc%d" % m)

    def put_z3(rows, value):
        gz_own[rows, :] = value + gc_r[3, rows, :].astype(F32)

    weight_part(z ^ 3, core, put_z3)
    arrived(gz_a, "za")
    gz_s[1, 0:512, :] = (gz_own[0:512, :] + gz_a[...].astype(F32)).astype(BF)
    gz_s[1, 512:1024, :] = gz_own[512:1024, :].astype(BF)
    send(gz_s.at[1], gz_r.at[1], "z3", to_seq(6))

    def put_z1(rows, value):
        gz_own[rows, :] = value + gc_r[1, rows, :].astype(F32)

    weight_part(z ^ 1, core, put_z1)
    arrived(gz_b, "zb")
    gz_s[2, 0:512, :] = gz_own[0:512, :].astype(BF)
    gz_s[2, 512:1024, :] = (gz_own[512:1024, :] + gz_b[...].astype(F32)).astype(BF)
    send(gz_s.at[2], gz_r.at[0], "z1", to_seq(2))

    def put_z0(rows, value):
        gz_own[rows, :] = value + gc_r[0, rows, :].astype(F32)

    weight_part(z, core, put_z0)

    arrived(g_recv, "g")

    def grad_total(b):
        rows = pl.ds(pl.multiple_of(b * 256, 256), 256)
        stage[0, rows, :] = (g_own[rows, :] + g_recv[rows, :].astype(F32)).astype(BF)

    loop(2, grad_total)
    permuted(stage.at[0], gp)

    def backward(level, h):
        n = R >> level
        keys = keys_of(level, h, 0)
        vals = keys_of(level, h, 1)
        grads = chosen(gp[h].astype(F32), level, h)
        factor = jnp.exp2(mms[level][h] - chosen(m_run[h], level, h)) * chosen(l_run[h], level, h)
        scaled = grads * factor
        delta = jnp.sum(scaled * chosen(attp[h].astype(F32), level, h), axis=1, keepdims=True)
        scaled = scaled.astype(BF)
        e = es[level][h]
        ds = (e.astype(F32) * (dot_t(scaled, vals) - delta)).astype(BF)
        dq = dot(ds, keys) * SCALE
        if level == 0:
            dqa[h] += dq
        elif level == 3:
            dqa[h] = placed(dq, level, h, 0.0)
        else:
            dqa[h] += placed(dq, level, h, 0.0)
        scaled_t = dot_t(eye[:DH, :DH], scaled).astype(BF)
        query_t = dot_t(eye[:DH, :DH], chosen_bf(qp[h], level, h)).astype(BF)
        dv_t = dot(scaled_t, e)
        dk_t = dot(query_t, ds) * SCALE
        both = dot_t(eye[...], jnp.concatenate([dk_t, dv_t], axis=0).astype(BF))
        if level == 0:
            dk0[h] = both[:, :DH]
            dv0[h] = both[:, DH:]
        else:
            shape = (1 << level, n, DH)
            snd[level][:, :, head_cols(h)] = both[:, :DH].astype(BF).reshape(shape)
            snd[level][:, :, head_cols(h + HL)] = both[:, DH:].astype(BF).reshape(shape)

    for level in (3, 2, 1, 0):
        loop(HL, lambda h, level=level: backward(level, h))
        if level > 0:
            me = s % (1 << level)
            for m in range((1 << level) - 1, 0, -1):
                send(snd[level].at[me ^ m], rcv[level].at[me], "b%d_%d" % (level, m), to_seq(m))

    def natural(dst):
        def tile(b):
            rows = pl.ds(pl.multiple_of(b * 256, 256), 256)
            dst[rows, :] = dot(unperm[rows, :], back[...]).astype(BF)

        loop(2, tile)

    for h in range(HL):
        back[:, h * DH : (h + 1) * DH] = dqa[h].astype(BF)
    natural(dq_o)

    arrived(res_r.at[0], "r1")
    arrived(res_r.at[1], "r3")

    def result_total(b):
        rows = pl.ds(pl.multiple_of(b * 128, 128), 128)
        res_o[rows, :] = (res_own[rows, :] + res_r[0, rows, :].astype(F32) + res_r[1, rows, :].astype(F32)).astype(BF)

    loop(4, result_total)

    arrived(gz_r.at[0], "z1")
    arrived(gz_r.at[1], "z3")
    for half_at in range(2):

        def weight_total(b, half_at=half_at):
            rows = pl.ds(pl.multiple_of(half_at * 512 + b * 128, 128), 128)
            total = gz_own[rows, :] + gz_r[0, rows, :].astype(F32) + gz_r[1, rows, :].astype(F32)
            gy_s[half_at, pl.ds(pl.multiple_of(b * 128, 128), 128), :] = total.astype(BF)

        loop(4, weight_total)
    def last_hop(half_at):
        i = ID["y0"]
        return pltpu.make_async_remote_copy(
            src_ref=gy_s.at[half_at], dst_ref=gy_r.at[yh], send_sem=ss.at[i + half_at], recv_sem=rs.at[i + yh],
            device_id=to_y(2 * q + half_at), device_id_type=pl.DeviceIdType.MESH,
        )

    for half_at in range(2):
        stays = (yh == q) & (q == half_at)

        @pl.when(stays)
        def _(half_at=half_at):
            gy_r[yh] = gy_s[half_at]

        @pl.when(jnp.logical_not(stays))
        def _(half_at=half_at):
            last_hop(half_at).start()

    for level in (3, 2, 1):
        me = s % (1 << level)
        for m in range((1 << level) - 1, 0, -1):
            arrived(rcv[level].at[me ^ m], "b%d_%d" % (level, m))

    for which, start_grad, dst in ((0, dk0, dk_o), (1, dv0, dv_o)):

        def key_total(h, which=which, start_grad=start_grad):
            total = start_grad[h]
            cols = head_cols(h + HL * which)
            for level in (1, 2, 3):
                me = s % (1 << level)
                owed = snd[level][me, :, cols].astype(F32)
                for m in range(1, 1 << level):
                    owed += rcv[level][me ^ m, :, cols].astype(F32)
                total += placed(owed, level, h, 0.0)
            back[:, head_cols(h)] = total.astype(BF)

        loop(HL, key_total)
        natural(dst)

    for source in range(2):

        @pl.when(jnp.logical_not((yh == source) & (q == yh)))
        def _(source=source):
            arrived(gy_r.at[source], "y%d" % source)

    gw_o[...] = (gy_r[0].astype(F32) + gy_r[1].astype(F32)).astype(BF)

    for half_at in range(2):

        @pl.when(jnp.logical_not((yh == q) & (q == half_at)))
        def _(half_at=half_at):
            last_hop(half_at).wait_send()

    for copy in sent:
        copy.wait_send()


def shards(queries, keys, values, offsets, out_weight, out_grad):
    wide = jax.ShapeDtypeStruct((R, C), BF)
    any_spec = pl.BlockSpec(memory_space=pl.ANY)
    vmem = pl.BlockSpec(memory_space=pltpu.VMEM)

    def bf(*shape):
        return pltpu.VMEM(shape, BF)

    def f32(*shape):
        return pltpu.VMEM(shape, F32)

    count = len(NAMES)
    return pl.pallas_call(
        kernel,
        out_shape=(wide, wide, wide, wide, jax.ShapeDtypeStruct((512, 256), BF)),
        in_specs=[pl.BlockSpec(memory_space=pltpu.SMEM)] + [any_spec] * 5,
        out_specs=[vmem] * 5,
        scratch_shapes=[
            bf(3, R, C), bf(R, R), bf(R, R), bf(R, R),
            bf(HL, R, DH), bf(HL, R, DH), bf(HL, R, DH),
            bf(2, 256, 1024), bf(4, 128, 1024), bf(8, 64, 1024),
            bf(HL, 512, R), bf(HL, 256, R), bf(HL, 128, R), bf(HL, 64, R),
            f32(HL, 512, DH), f32(HL, 256, DH), f32(HL, 128, DH), f32(HL, 64, DH),
            f32(HL, R, DH), f32(HL, R, DH), f32(HL, R, DH),
            bf(HL, R, DH), bf(2, R, C), bf(1024, R),
            bf(4, R, C), bf(2, C, 2048),
            f32(R, C), bf(R, C), bf(R, C), bf(HL, R, DH),
            bf(3, R, C), bf(256, C), bf(256, C), bf(2, R, C), f32(R, C),
            bf(4, 1024, 256), bf(4, 1024, 256),
            bf(3, 1024, 256), bf(512, 256), bf(512, 256), bf(2, 1024, 256), f32(1024, 256),
            bf(2, 512, 256), bf(2, 512, 256),
            f32(HL, R, DH), f32(HL, R, DH), f32(HL, R, DH),
            bf(2, 256, 1024), bf(4, 128, 1024), bf(8, 64, 1024),
            bf(2, 256, 1024), bf(4, 128, 1024), bf(8, 64, 1024),
            bf(R, C),
            pltpu.SemaphoreType.DMA((count,)), pltpu.SemaphoreType.DMA((count,)), pltpu.SemaphoreType.DMA((5,)),
        ],
        compiler_params=pltpu.CompilerParams(
            collective_id=0, has_side_effects=True, vmem_limit_bytes=60 * 1024 * 1024
        ),
    )(offsets, queries, keys, values, out_weight, out_grad)


def solution(mesh):
    return jax.shard_map(
        shards,
        mesh=mesh,
        in_specs=(
            P("seq", "tp"),
            P("seq", "tp"),
            P("seq", "tp"),
            P(),
            P("tp", None),
            P("seq", "tp"),
        ),
        out_specs=(P("seq", "tp"), P("seq", "tp"), P("seq", "tp"), P("seq", "tp"), P("tp", "seq")),
        check_vma=False,
    )
```

```python
import jax
import jax.numpy as jnp
from jax import lax
from jax.experimental import pallas as pl
from jax.experimental.pallas import tpu as pltpu
from jax.sharding import PartitionSpec as P

DH = 128
LEV = 3
R = 512
C = 512
HL = 4
SCALE = DH**-0.5
K2E = SCALE * 1.4426950408889634
NEG = -1e30
BF = jnp.bfloat16
F32 = jnp.float32

NAMES = (
    ["og1", "og3", "ogA", "ogB", "w", "wf"]
    + ["kvo1", "kvo2", "kvo3", "kv2", "kvf2"]
    + ["kv3_1", "kv3_2", "kv3_3", "kvf3_1", "kvf3_2", "kvf3_3"]
    + ["att0", "att1", "att2", "att3", "g"]
    + ["ra", "rb", "r1", "r3"]
    + ["%s%d" % (name, hb) for hb in range(2) for name in ("gcA", "gcB", "za", "zb", "z1", "z3")]
    + ["y0", "y1", "c1", "c2", "c3", "b2_1", "b3_1", "b3_2", "b3_3"]
)
ID = {name: i for i, name in enumerate(NAMES)}


def dot(a, b):
    return lax.dot_general(a, b, (((1,), (0,)), ((), ())), preferred_element_type=F32)


def dot_t(a, b):
    return lax.dot_general(a, b, (((1,), (1,)), ((), ())), preferred_element_type=F32)


def heads(body):
    for h in range(HL):
        body(h)


def loop(count, body):
    def step(i, carry):
        body(i)
        return carry

    lax.fori_loop(0, count, step, 0)


def kernel(
    offs, q_hbm, k_hbm, v_hbm, w_hbm, og_hbm,
    res_o, dq_o, dk_o, dv_o, gw_o,
    stage, perm, unperm, eye, qp, kp, vp, kv1, kv2, kv3, e0, e1, e2, e3, mm0, mm1, mm2, mm3,
    m_run, l_run, n_run, attp, att_buf, att_t, og_buf, wblk, g_own, g_send, g_recv, gp,
    res_s, res_a, res_b, res_r, res_f, gc_s, gc_r, gz_s, gz_a, gz_b, gz_r, gz_f, gy_s, gy_r,
    dqa, dk0, dv0, snd1, snd2, snd3, cr1, cr2, cr3, zs2, zs3, rz2, rz3, back,
    ss, rs, ls,
):
    s = lax.axis_index("seq")
    t = lax.axis_index("tp")
    core = s % 2
    z = (s // 2) % 4
    yh = s // 8
    x = t % 4
    q = t // 4
    y = 2 * yh + q
    s_base = yh * 8
    s8 = s % 8
    kv = [None, kv1, kv2, kv3]
    es = [e0, e1, e2, e3]
    mms = [mm0, mm1, mm2, mm3]
    snd = [None, snd1, snd2, snd3]
    sent = []

    def to_seq(mask):
        return (s_base + (s8 ^ mask), t)

    def to_x(mask):
        return (s, q * 4 + (x ^ mask))

    def to_y(yy):
        return ((yy // 2) * 8 + s8, (yy % 2) * 4 + x)

    def remote(src, dst, name, device, extra=0):
        i = ID[name] + extra
        return pltpu.make_async_remote_copy(
            src_ref=src, dst_ref=dst, send_sem=ss.at[i], recv_sem=rs.at[i],
            device_id=device, device_id_type=pl.DeviceIdType.MESH,
        )

    def send(src, dst, name, device):
        copy = remote(src, dst, name, device)
        copy.start()
        sent.append(copy)

    def arrived(dst, name):
        remote(dst, dst, name, to_seq(1)).wait_recv()

    def head_cols(h):
        return pl.ds(h * DH, DH)

    def local(src, dst, i):
        copy = pltpu.make_async_copy(src, dst, ls.at[i])
        copy.start()
        return copy

    barrier = pltpu.get_barrier_semaphore()
    peers = [to_seq(m) for m in range(1, 8)] + [to_x(1), to_x(3)] + [to_y((y + d) % 4) for d in (1, 2, 3)]
    for peer in peers:
        pl.semaphore_signal(barrier, inc=1, device_id=peer, device_id_type=pl.DeviceIdType.MESH)
    k_in = local(k_hbm, stage.at[0], 0)
    v_in = local(v_hbm, stage.at[1], 1)
    q_in = local(q_hbm, stage.at[2], 2)
    og_in = local(og_hbm, og_buf.at[x], 3)
    half = pl.ds(pl.multiple_of(q * 2048, 2048), 2048)
    w_in = local(w_hbm.at[:, half], wblk.at[q], 4)


    def place_of(i):
        return ((i & 1) << 8) | (((i >> 1) & 1) << 7) | (((i >> 2) & 1) << 6) | (i >> 3)

    rows_i = lax.broadcasted_iota(jnp.int32, (R, R), 0)
    cols_i = lax.broadcasted_iota(jnp.int32, (R, R), 1)
    perm[...] = jnp.where(rows_i == place_of(cols_i), 1.0, 0.0).astype(BF)
    pl.semaphore_wait(barrier, len(peers))

    send(og_hbm, og_buf.at[x], "og1", to_x(1))
    send(og_hbm, og_buf.at[x], "og3", to_x(3))
    w_there = pl.ds(pl.multiple_of((1 - q) * 2048 + core * 1024, 1024), 1024)
    w_mine = pl.ds(pl.multiple_of(core * 1024, 1024), 1024)
    w_other = pl.ds(pl.multiple_of((1 - core) * 1024, 1024), 1024)
    send(w_hbm.at[:, w_there], wblk.at[q, :, w_mine], "w", to_y((y + 3 + 2 * core) % 4))

    def permuted(src, dst):
        def tile(b):
            rows = pl.ds(pl.multiple_of(b * 256, 256), 256)
            moved = dot(perm[rows, :], src[...]).astype(BF)
            for h in range(HL):
                dst[h, rows, :] = moved[:, h * DH : (h + 1) * DH]

        loop(2, tile)

    def phase_of(level, h):
        return offs[level - 1, t * HL + h]

    def chosen(value, level, h):
        for bit in range(level):
            n = value.shape[0] // 2
            flag = jnp.full((n, DH), (phase_of(level, h) >> bit) & 1, jnp.int32)
            value = jnp.where(flag == 1, value[n:], value[:n])
        return value

    def chosen_bf(value, level, h):
        return value if level == 0 else chosen(value.astype(F32), level, h).astype(BF)

    unperm[...] = jnp.where(cols_i == place_of(rows_i), 1.0, 0.0).astype(BF)
    eye[...] = jnp.where(rows_i == cols_i, 1.0, 0.0).astype(BF)
    k_in.wait()
    permuted(stage.at[0], kp)
    v_in.wait()
    permuted(stage.at[1], vp)
    for level in (3, 2, 1):
        n = R >> level
        slot = s % (1 << level)

        def fill(h, level=level, n=n, slot=slot):
            kv[level][slot, :, head_cols(h)] = chosen_bf(kp[h], level, h)
            kv[level][slot, :, head_cols(h + HL)] = chosen_bf(vp[h], level, h)

        heads(fill)
        mine = kv[level].at[slot]
        if level == 3:
            for m in (2, 1, 3):
                send(mine, mine, "kv3_%d" % m, to_seq(2 * m))
        if level == 2:
            send(mine, mine, "kv2", to_seq(2))
        send(mine, mine, "kvo%d" % level, to_seq(1))
    q_in.wait()
    permuted(stage.at[2], qp)

    def placed(value, level, h, fill):
        phase = jnp.full(value.shape, phase_of(level, h), jnp.int32)
        order = [sum(((p >> (level - 1 - bit)) & 1) << bit for bit in range(level)) for p in range(1 << level)]
        return jnp.concatenate([jnp.where(phase == p, value, fill) for p in order], axis=0)

    def keys_of(level, h, which):
        if level == 0:
            return (kp, vp)[which][h]
        return kv[level][:, :, head_cols(h + HL * which)].reshape(R, DH)

    def forward(level, h):
        n = R >> level
        rows = min(n, 256)
        keys = keys_of(level, h, 0)
        vals = jnp.concatenate([keys_of(level, h, 1), jnp.ones((R, DH), BF)], axis=1)
        for b in range(0, n, rows):
            if level == 0:
                queries = qp[h, b : b + rows, :]
            else:
                queries = chosen_bf(qp[h], level, h)
            scores = dot_t(queries, keys) * K2E
            top = jnp.max(scores, axis=1, keepdims=True)
            e = jnp.exp2(scores - top).astype(BF)
            es[level][h, b : b + rows, :] = e
            nl = dot(e, vals)
            top = jnp.broadcast_to(top, (rows, DH))
            mms[level][h, b : b + rows, :] = top
            if level == 0:
                m_run[h, b : b + rows, :] = top
                n_run[h, b : b + rows, :] = nl[:, :DH]
                l_run[h, b : b + rows, :] = nl[:, DH:]
        if level > 0:
            old = m_run[h]
            this = placed(top, level, h, NEG)
            new = jnp.maximum(old, this)
            a_old = jnp.exp2(old - new)
            a_this = jnp.exp2(this - new)
            m_run[h] = new
            n_run[h] = n_run[h] * a_old + a_this * jnp.concatenate([nl[:, :DH]] * (1 << level), axis=0)
            l_run[h] = l_run[h] * a_old + a_this * jnp.concatenate([nl[:, DH:]] * (1 << level), axis=0)

    heads(lambda h: forward(0, h))

    s4 = s % 4
    there = kv2.at[s4 ^ 2]
    arrived(there, "kv2")
    send(there, there, "kvf2", to_seq(1))
    arrived(kv1.at[core ^ 1], "kvo1")
    heads(lambda h: forward(1, h))
    for m in (1, 3, 2):
        there = kv3.at[s8 ^ (2 * m)]
        arrived(there, "kv3_%d" % m)
        send(there, there, "kvf3_%d" % m, to_seq(1))
    arrived(kv2.at[s4 ^ 1], "kvo2")
    arrived(kv2.at[s4 ^ 3], "kvf2")
    arrived(og_buf.at[x ^ 1], "og1")
    send(og_buf.at[x ^ 1, 0:256], og_buf.at[x ^ 1, 0:256], "ogA", to_x(3))
    arrived(og_buf.at[x ^ 3], "og3")
    send(og_buf.at[x ^ 3, 256:512], og_buf.at[x ^ 3, 256:512], "ogB", to_x(1))
    w_got = wblk.at[1 - q, :, w_mine]
    arrived(w_got, "w")
    send(w_got, w_got, "wf", to_seq(1))

    heads(lambda h: forward(2, h))

    arrived(kv3.at[s8 ^ 1], "kvo3")
    for m in (1, 3, 2):
        arrived(kv3.at[s8 ^ (2 * m + 1)], "kvf3_%d" % m)

    def last_level(h):
        forward(3, h)
        inverse = 1.0 / l_run[h]
        l_run[h] = inverse
        attended = (n_run[h] * inverse).astype(BF)
        attp[h] = attended
        att_buf[q, :, head_cols(h)] = dot(unperm[...], attended).astype(BF)
        block = att_buf.at[q, :, head_cols(h)]
        remote(block, block, "att0", to_y(y ^ 1), extra=h).start()

    heads(last_level)
    for h in range(HL):
        block = att_buf.at[q, :, h * DH : (h + 1) * DH]
        sent.append(remote(block, block, "att%d" % h, to_y(y ^ 1)))

    og_in.wait()
    w_in.wait()
    arrived(og_buf.at[x ^ 2, 0:256], "ogA")
    arrived(og_buf.at[x ^ 2, 256:512], "ogB")
    arrived(wblk.at[1 - q, :, w_other], "wf")

    def grad_part(which, dst):
        def tile(b):
            rows = pl.ds(pl.multiple_of(b * 256, 256), 256)
            total = dot_t(og_buf[0, rows, :], wblk[which, :, 0:512])
            for xx in range(1, 4):
                total += dot_t(og_buf[xx, rows, :], wblk[which, :, xx * 512 : (xx + 1) * 512])
            dst[rows, :] = total.astype(dst.dtype)

        loop(2, tile)

    grad_part(1 - q, g_send)
    send(g_send, g_recv, "g", to_y(y ^ 1))

    order = (2, 3, 1, 0)

    def transposed(hb, which):
        for h in range(HL):
            att_t[hb, h * DH : (h + 1) * DH, :] = dot_t(eye[:DH, :DH], att_buf[which, :, h * DH : (h + 1) * DH]).astype(BF)

    def weight_part(hb, i, cc):
        cols = pl.ds(pl.multiple_of(cc * 256, 256), 256)
        return dot(att_t[hb], og_buf[z ^ order[i], :, cols])

    def weight_first(hb):
        for i in range(4):
            gc_s[hb, i] = weight_part(hb, i, 1 - core).astype(BF)
            if i == 0:
                send(gc_s.at[hb, 0], gc_r.at[hb, 0], "gcA%d" % hb, to_seq(1))
        send(gc_s.at[hb, 1:4], gc_r.at[hb, 1:4], "gcB%d" % hb, to_seq(1))

    def weight_second(hb):
        arrived(gc_r.at[hb, 0], "gcA%d" % hb)
        gz_s[hb, 0] = (weight_part(hb, 0, core) + gc_r[hb, 0].astype(F32)).astype(BF)
        send(gz_s.at[hb, 0, 0:256], gz_a.at[hb], "za%d" % hb, to_seq(2))
        send(gz_s.at[hb, 0, 256:512], gz_b.at[hb], "zb%d" % hb, to_seq(6))
        arrived(gc_r.at[hb, 1:4], "gcB%d" % hb)
        for i in range(1, 4):
            gz_f[hb, i - 1] = weight_part(hb, i, core) + gc_r[hb, i].astype(F32)

    def weight_third(hb):
        arrived(gz_a.at[hb], "za%d" % hb)
        gz_s[hb, 1, 0:256, :] = (gz_f[hb, 0, 0:256, :] + gz_a[hb].astype(F32)).astype(BF)
        gz_s[hb, 1, 256:512, :] = gz_f[hb, 0, 256:512, :].astype(BF)
        send(gz_s.at[hb, 1], gz_r.at[hb, 1], "z3%d" % hb, to_seq(6))
        arrived(gz_b.at[hb], "zb%d" % hb)
        gz_s[hb, 2, 0:256, :] = gz_f[hb, 1, 0:256, :].astype(BF)
        gz_s[hb, 2, 256:512, :] = (gz_f[hb, 1, 256:512, :] + gz_b[hb].astype(F32)).astype(BF)
        send(gz_s.at[hb, 2], gz_r.at[hb, 0], "z1%d" % hb, to_seq(2))

    def last_hop(hb):
        i = ID["y0"]
        return pltpu.make_async_remote_copy(
            src_ref=gy_s.at[hb], dst_ref=gy_r.at[yh], send_sem=ss.at[i + hb], recv_sem=rs.at[i + yh],
            device_id=to_y(3 * q if hb == 0 else q + 1), device_id_type=pl.DeviceIdType.MESH,
        )

    def weight_fourth(hb):
        arrived(gz_r.at[hb, 0], "z1%d" % hb)
        arrived(gz_r.at[hb, 1], "z3%d" % hb)
        total = gz_f[hb, 2] + gz_r[hb, 0].astype(F32) + gz_r[hb, 1].astype(F32)
        gy_s[hb] = total.astype(BF)
        if hb == 1:
            last_hop(1).start()
            return

        @pl.when(yh == q)
        def _():
            gy_r[yh] = gy_s[0]

        @pl.when(yh != q)
        def _():
            last_hop(0).start()

    def result_part(i):
        cols = pl.ds(pl.multiple_of((x ^ order[i]) * 512, 512), 512)
        return dot(att_buf[0], wblk[0, :, cols]) + dot(att_buf[1], wblk[1, :, cols])

    transposed(0, q)
    weight_first(0)
    grad_part(q, g_own)
    weight_second(0)

    for h in range(HL):
        arrived(att_buf.at[1 - q, :, h * DH : (h + 1) * DH], "att%d" % h)
    res_s[0] = result_part(0).astype(BF)
    send(res_s.at[0, 0:256], res_a, "ra", to_x(1))
    send(res_s.at[0, 256:512], res_b, "rb", to_x(3))
    transposed(1, 1 - q)
    weight_first(1)
    for i in range(1, 4):
        res_f[i - 1] = result_part(i)
    weight_third(0)
    weight_second(1)
    arrived(res_a, "ra")
    res_s[1, 0:256, :] = (res_f[0, 0:256, :] + res_a[...].astype(F32)).astype(BF)
    res_s[1, 256:512, :] = res_f[0, 256:512, :].astype(BF)
    send(res_s.at[1], res_r.at[1], "r3", to_x(3))
    arrived(res_b, "rb")
    res_s[2, 0:256, :] = res_f[1, 0:256, :].astype(BF)
    res_s[2, 256:512, :] = (res_f[1, 256:512, :] + res_b[...].astype(F32)).astype(BF)
    send(res_s.at[2], res_r.at[0], "r1", to_x(1))
    weight_third(1)

    arrived(g_recv, "g")

    def grad_total(b):
        rows = pl.ds(pl.multiple_of(b * 256, 256), 256)
        stage[0, rows, :] = (g_own[rows, :] + g_recv[rows, :].astype(F32)).astype(BF)

    loop(2, grad_total)
    permuted(stage.at[0], gp)

    def backward(level, h):
        n = R >> level
        keys = keys_of(level, h, 0)
        vals = keys_of(level, h, 1)
        grads = chosen(gp[h].astype(F32), level, h)
        factor = jnp.exp2(mms[level][h] - chosen(m_run[h], level, h)) * chosen(l_run[h], level, h)
        scaled = grads * factor
        delta = jnp.sum(scaled * chosen(attp[h].astype(F32), level, h), axis=1, keepdims=True)
        scaled = scaled.astype(BF)
        e = es[level][h]
        ds = (e.astype(F32) * (dot_t(scaled, vals) - delta)).astype(BF)
        dq = dot(ds, keys) * SCALE
        if level == 0:
            dqa[h] += dq
        elif level == 3:
            dqa[h] = placed(dq, level, h, 0.0)
        else:
            dqa[h] += placed(dq, level, h, 0.0)
        scaled_t = dot_t(eye[:DH, :DH], scaled).astype(BF)
        query_t = dot_t(eye[:DH, :DH], chosen_bf(qp[h], level, h)).astype(BF)
        dv_t = dot(scaled_t, e)
        dk_t = dot(query_t, ds) * SCALE
        both = dot_t(eye[...], jnp.concatenate([dk_t, dv_t], axis=0).astype(BF))
        if level == 0:
            dk0[h] = both[:, :DH]
            dv0[h] = both[:, DH:]
        else:
            shape = snd[level].shape[:-1] + (DH,)
            snd[level][..., head_cols(h)] = both[:, :DH].astype(BF).reshape(shape)
            snd[level][..., head_cols(h + HL)] = both[:, DH:].astype(BF).reshape(shape)

    zb = z % 2
    heads(lambda h: backward(3, h))
    send(snd3.at[:, 1 - core], cr3, "c3", to_seq(1))
    heads(lambda h: backward(2, h))
    send(snd2.at[:, 1 - core], cr2, "c2", to_seq(1))
    arrived(cr3, "c3")
    for m in (2, 1, 3):
        zs3[m - 1] = (snd3[z ^ m, core].astype(F32) + cr3[z ^ m].astype(F32)).astype(BF)
        send(zs3.at[m - 1], rz3.at[m - 1], "b3_%d" % m, to_seq(2 * m))
    heads(lambda h: backward(1, h))
    send(snd1.at[1 - core], cr1, "c1", to_seq(1))
    arrived(cr2, "c2")
    zs2[...] = (snd2[zb ^ 1, core].astype(F32) + cr2[zb ^ 1].astype(F32)).astype(BF)
    send(zs2, rz2, "b2_1", to_seq(2))
    weight_fourth(0)
    heads(lambda h: backward(0, h))

    def natural(dst):
        def tile(b):
            rows = pl.ds(pl.multiple_of(b * 256, 256), 256)
            dst[rows, :] = dot(unperm[rows, :], back[...]).astype(BF)

        loop(2, tile)

    for h in range(HL):
        back[:, h * DH : (h + 1) * DH] = dqa[h].astype(BF)
    natural(dq_o)

    arrived(res_r.at[0], "r1")
    arrived(res_r.at[1], "r3")

    def result_total(b):
        rows = pl.ds(pl.multiple_of(b * 128, 128), 128)
        res_o[rows, :] = (res_f[2, rows, :] + res_r[0, rows, :].astype(F32) + res_r[1, rows, :].astype(F32)).astype(BF)

    loop(4, result_total)
    weight_fourth(1)

    arrived(cr1, "c1")
    for m in (1, 3, 2):
        arrived(rz3.at[m - 1], "b3_%d" % m)
    arrived(rz2, "b2_1")

    for which, start_grad, dst in ((0, dk0, dk_o), (1, dv0, dv_o)):

        def key_total(h, which=which, start_grad=start_grad):
            total = start_grad[h]
            cols = head_cols(h + HL * which)
            owed = snd1[core, :, cols].astype(F32) + cr1[:, cols].astype(F32)
            total += placed(owed, 1, h, 0.0)
            owed = snd2[zb, core, :, cols].astype(F32) + cr2[zb, :, cols].astype(F32) + rz2[:, cols].astype(F32)
            total += placed(owed, 2, h, 0.0)
            owed = snd3[z, core, :, cols].astype(F32) + cr3[z, :, cols].astype(F32)
            for m in range(3):
                owed += rz3[m, :, cols].astype(F32)
            total += placed(owed, 3, h, 0.0)
            back[:, head_cols(h)] = total.astype(BF)

        heads(key_total)
        natural(dst)

    for source in range(2):

        @pl.when(jnp.logical_not((yh == source) & (q == yh)))
        def _(source=source):
            arrived(gy_r.at[source], "y%d" % source)

    gw_o[...] = (gy_r[0].astype(F32) + gy_r[1].astype(F32)).astype(BF)

    last_hop(1).wait_send()

    @pl.when(yh != q)
    def _():
        last_hop(0).wait_send()

    for copy in sent:
        copy.wait_send()


def hand_over(*refs):
    copies = [pltpu.make_async_copy(refs[i], refs[5 + i], refs[10].at[i]) for i in range(5)]
    for copy in copies:
        copy.start()
    for copy in copies:
        copy.wait()


def shards(queries, keys, values, offsets, out_weight, out_grad):
    wide = jax.ShapeDtypeStruct((R, C), BF)
    any_spec = pl.BlockSpec(memory_space=pl.ANY)
    vmem = pl.BlockSpec(memory_space=pltpu.VMEM)

    def bf(*shape):
        return pltpu.VMEM(shape, BF)

    def f32(*shape):
        return pltpu.VMEM(shape, F32)

    count = len(NAMES)
    outs = (wide, wide, wide, wide, jax.ShapeDtypeStruct((512, 256), BF))
    made = pl.pallas_call(
        kernel,
        out_shape=outs,
        in_specs=[pl.BlockSpec(memory_space=pltpu.SMEM)] + [any_spec] * 5,
        out_specs=[vmem] * 5,
        scratch_shapes=[
            bf(3, R, C), bf(R, R), bf(R, R), bf(R, R),
            bf(HL, R, DH), bf(HL, R, DH), bf(HL, R, DH),
            bf(2, 256, 1024), bf(4, 128, 1024), bf(8, 64, 1024),
            bf(HL, 512, R), bf(HL, 256, R), bf(HL, 128, R), bf(HL, 64, R),
            f32(HL, 512, DH), f32(HL, 256, DH), f32(HL, 128, DH), f32(HL, 64, DH),
            f32(HL, R, DH), f32(HL, R, DH), f32(HL, R, DH),
            bf(HL, R, DH), bf(2, R, C), bf(2, C, R),
            bf(4, R, C), bf(2, C, 2048),
            f32(R, C), bf(R, C), bf(R, C), bf(HL, R, DH),
            bf(3, R, C), bf(256, C), bf(256, C), bf(2, R, C), f32(3, R, C),
            bf(2, 4, C, 256), bf(2, 4, C, 256),
            bf(2, 3, C, 256), bf(2, 256, 256), bf(2, 256, 256), bf(2, 2, C, 256), f32(2, 3, C, 256),
            bf(2, 512, 256), bf(2, 512, 256),
            f32(HL, R, DH), f32(HL, R, DH), f32(HL, R, DH),
            bf(2, 256, 1024), bf(2, 2, 128, 1024), bf(4, 2, 64, 1024),
            bf(256, 1024), bf(2, 128, 1024), bf(4, 64, 1024),
            bf(128, 1024), bf(3, 64, 1024), bf(128, 1024), bf(3, 64, 1024),
            bf(R, C),
            pltpu.SemaphoreType.DMA((count,)), pltpu.SemaphoreType.DMA((count,)), pltpu.SemaphoreType.DMA((5,)),
        ],
        compiler_params=pltpu.CompilerParams(
            collective_id=0, has_side_effects=True, vmem_limit_bytes=60 * 1024 * 1024
        ),
    )(offsets, queries, keys, values, out_weight, out_grad)
    return pl.pallas_call(
        hand_over, out_shape=outs, in_specs=[any_spec] * 5, out_specs=[any_spec] * 5,
        scratch_shapes=[pltpu.SemaphoreType.DMA((5,))],
        compiler_params=pltpu.CompilerParams(vmem_limit_bytes=60 * 1024 * 1024),
    )(*made)


def solution(mesh):
    return jax.shard_map(
        shards,
        mesh=mesh,
        in_specs=(
            P("seq", "tp"),
            P("seq", "tp"),
            P("seq", "tp"),
            P(),
            P("tp", None),
            P("seq", "tp"),
        ),
        out_specs=(P("seq", "tp"), P("seq", "tp"), P("seq", "tp"), P("seq", "tp"), P("tp", "seq")),
        check_vma=False,
    )
```

```python
import jax
import jax.numpy as jnp
from jax import lax
from jax.experimental import pallas as pl
from jax.experimental.pallas import tpu as pltpu
from jax.sharding import PartitionSpec as P

DH = 128
LEV = 3
R = 512
C = 512
HL = 4
SCALE = DH**-0.5
K2E = SCALE * 1.4426950408889634
NEG = -1e30
BF = jnp.bfloat16
F32 = jnp.float32

NAMES = (
    ["og1", "og3", "ogA", "ogB", "w", "wf"]
    + ["kvo1", "kvo2", "kvo3", "kv2", "kvf2"]
    + ["kv3_1", "kv3_2", "kv3_3", "kvf3_1", "kvf3_2", "kvf3_3"]
    + ["att0", "att1", "att2", "att3", "g"]
    + ["ra", "rb", "r1", "r3"]
    + ["%s%d" % (name, hb) for hb in range(2) for name in ("gcA", "gcB", "za", "zb", "z1", "z3")]
    + ["y0", "y1", "c1", "c2", "c3", "b2_1", "b3_1", "b3_2", "b3_3"]
)
ID = {name: i for i, name in enumerate(NAMES)}


def dot(a, b):
    return lax.dot_general(a, b, (((1,), (0,)), ((), ())), preferred_element_type=F32)


def dot_t(a, b):
    return lax.dot_general(a, b, (((1,), (1,)), ((), ())), preferred_element_type=F32)


def heads(body):
    for h in range(HL):
        body(h)


def loop(count, body):
    def step(i, carry):
        body(i)
        return carry

    lax.fori_loop(0, count, step, 0)


def kernel(
    offs, q_hbm, k_hbm, v_hbm, w_hbm, og_hbm,
    res_o, dq_o, dk_o, dv_o, gw_o,
    stage, perm, unperm, eye, qp, kp, vp, kv1, kv2, kv3, e0, e1, e2, e3, mm0, mm1, mm2, mm3,
    m_run, l_run, n_run, attp, att_buf, att_t, og_buf, wblk, g_own, g_send, g_recv, gp,
    res_s, res_a, res_b, res_r, res_f, gc_s, gc_r, gz_s, gz_a, gz_b, gz_r, gz_f, gy_s, gy_r,
    dqa, dk0, dv0, snd1, snd2, snd3, cr1, cr2, cr3, zs2, zs3, rz2, rz3, back,
    ss, rs, ls,
):
    s = lax.axis_index("seq")
    t = lax.axis_index("tp")
    core = s % 2
    z = (s // 2) % 4
    yh = s // 8
    x = t % 4
    q = t // 4
    y = 2 * yh + q
    s_base = yh * 8
    s8 = s % 8
    kv = [None, kv1, kv2, kv3]
    es = [e0, e1, e2, e3]
    mms = [mm0, mm1, mm2, mm3]
    snd = [None, snd1, snd2, snd3]
    sent = []

    def to_seq(mask):
        return (s_base + (s8 ^ mask), t)

    def to_x(mask):
        return (s, q * 4 + (x ^ mask))

    def to_y(yy):
        return ((yy // 2) * 8 + s8, (yy % 2) * 4 + x)

    def remote(src, dst, name, device, extra=0):
        i = ID[name] + extra
        return pltpu.make_async_remote_copy(
            src_ref=src, dst_ref=dst, send_sem=ss.at[i], recv_sem=rs.at[i],
            device_id=device, device_id_type=pl.DeviceIdType.MESH,
        )

    def send(src, dst, name, device):
        copy = remote(src, dst, name, device)
        copy.start()
        sent.append(copy)

    def arrived(dst, name):
        remote(dst, dst, name, to_seq(1)).wait_recv()

    def head_cols(h):
        return pl.ds(h * DH, DH)

    def local(src, dst, i):
        copy = pltpu.make_async_copy(src, dst, ls.at[i])
        copy.start()
        return copy

    barrier = pltpu.get_barrier_semaphore()
    peers = [to_seq(m) for m in range(1, 8)] + [to_x(1), to_x(3)] + [to_y((y + d) % 4) for d in (1, 2, 3)]
    for peer in peers:
        pl.semaphore_signal(barrier, inc=1, device_id=peer, device_id_type=pl.DeviceIdType.MESH)
    k_in = local(k_hbm, stage.at[0], 0)
    v_in = local(v_hbm, stage.at[1], 1)
    q_in = local(q_hbm, stage.at[2], 2)
    og_in = local(og_hbm, og_buf.at[x], 3)
    half = pl.ds(pl.multiple_of(q * 2048, 2048), 2048)
    w_in = local(w_hbm.at[:, half], wblk.at[q], 4)


    def place_of(i):
        return ((i & 1) << 8) | (((i >> 1) & 1) << 7) | (((i >> 2) & 1) << 6) | (i >> 3)

    rows_i = lax.broadcasted_iota(jnp.int32, (R, R), 0)
    cols_i = lax.broadcasted_iota(jnp.int32, (R, R), 1)
    perm[...] = jnp.where(rows_i == place_of(cols_i), 1.0, 0.0).astype(BF)
    pl.semaphore_wait(barrier, len(peers))

    send(og_hbm, og_buf.at[x], "og1", to_x(1))
    send(og_hbm, og_buf.at[x], "og3", to_x(3))
    w_there = pl.ds(pl.multiple_of((1 - q) * 2048 + core * 1024, 1024), 1024)
    w_mine = pl.ds(pl.multiple_of(core * 1024, 1024), 1024)
    w_other = pl.ds(pl.multiple_of((1 - core) * 1024, 1024), 1024)
    send(w_hbm.at[:, w_there], wblk.at[q, :, w_mine], "w", to_y((y + 3 + 2 * core) % 4))

    def permuted(src, dst):
        def tile(b):
            rows = pl.ds(pl.multiple_of(b * 256, 256), 256)
            moved = dot(perm[rows, :], src[...]).astype(BF)
            for h in range(HL):
                dst[h, rows, :] = moved[:, h * DH : (h + 1) * DH]

        loop(2, tile)

    def phase_of(level, h):
        return offs[level - 1, t * HL + h]

    def chosen(value, level, h):
        for bit in range(level):
            n = value.shape[0] // 2
            flag = jnp.full((n, DH), (phase_of(level, h) >> bit) & 1, jnp.int32)
            value = jnp.where(flag == 1, value[n:], value[:n])
        return value

    def chosen_bf(value, level, h):
        return value if level == 0 else chosen(value.astype(F32), level, h).astype(BF)

    unperm[...] = jnp.where(cols_i == place_of(rows_i), 1.0, 0.0).astype(BF)
    eye[...] = jnp.where(rows_i == cols_i, 1.0, 0.0).astype(BF)
    k_in.wait()
    permuted(stage.at[0], kp)
    v_in.wait()
    permuted(stage.at[1], vp)
    for level in (3, 2, 1):
        n = R >> level
        slot = s % (1 << level)

        def fill(h, level=level, n=n, slot=slot):
            kv[level][slot, :, head_cols(h)] = chosen_bf(kp[h], level, h)
            kv[level][slot, :, head_cols(h + HL)] = chosen_bf(vp[h], level, h)

        heads(fill)
        mine = kv[level].at[slot]
        if level == 3:
            for m in (2, 1, 3):
                send(mine, mine, "kv3_%d" % m, to_seq(2 * m))
        if level == 2:
            send(mine, mine, "kv2", to_seq(2))
        send(mine, mine, "kvo%d" % level, to_seq(1))
    q_in.wait()
    permuted(stage.at[2], qp)

    def placed(value, level, h, fill):
        phase = jnp.full(value.shape, phase_of(level, h), jnp.int32)
        order = [sum(((p >> (level - 1 - bit)) & 1) << bit for bit in range(level)) for p in range(1 << level)]
        return jnp.concatenate([jnp.where(phase == p, value, fill) for p in order], axis=0)

    def keys_of(level, h, which):
        if level == 0:
            return (kp, vp)[which][h]
        return kv[level][:, :, head_cols(h + HL * which)].reshape(R, DH)

    def forward(level, h):
        n = R >> level
        rows = min(n, 256)
        keys = keys_of(level, h, 0)
        vals = jnp.concatenate([keys_of(level, h, 1), jnp.ones((R, DH), BF)], axis=1)
        for b in range(0, n, rows):
            if level == 0:
                queries = qp[h, b : b + rows, :]
            else:
                queries = chosen_bf(qp[h], level, h)
            scores = dot_t(queries, keys) * K2E
            top = jnp.max(scores, axis=1, keepdims=True)
            e = jnp.exp2(scores - top).astype(BF)
            es[level][h, b : b + rows, :] = e
            nl = dot(e, vals)
            top = jnp.broadcast_to(top, (rows, DH))
            mms[level][h, b : b + rows, :] = top
            if level == 0:
                m_run[h, b : b + rows, :] = top
                n_run[h, b : b + rows, :] = nl[:, :DH]
                l_run[h, b : b + rows, :] = nl[:, DH:]
        if level > 0:
            old = m_run[h]
            this = placed(top, level, h, NEG)
            new = jnp.maximum(old, this)
            a_old = jnp.exp2(old - new)
            a_this = jnp.exp2(this - new)
            m_run[h] = new
            n_run[h] = n_run[h] * a_old + a_this * jnp.concatenate([nl[:, :DH]] * (1 << level), axis=0)
            l_run[h] = l_run[h] * a_old + a_this * jnp.concatenate([nl[:, DH:]] * (1 << level), axis=0)

    heads(lambda h: forward(0, h))

    s4 = s % 4
    there = kv2.at[s4 ^ 2]
    arrived(there, "kv2")
    send(there, there, "kvf2", to_seq(1))
    arrived(kv1.at[core ^ 1], "kvo1")
    heads(lambda h: forward(1, h))
    for m in (1, 3, 2):
        there = kv3.at[s8 ^ (2 * m)]
        arrived(there, "kv3_%d" % m)
        send(there, there, "kvf3_%d" % m, to_seq(1))
    arrived(kv2.at[s4 ^ 1], "kvo2")
    arrived(kv2.at[s4 ^ 3], "kvf2")
    arrived(og_buf.at[x ^ 1], "og1")
    send(og_buf.at[x ^ 1, 0:256], og_buf.at[x ^ 1, 0:256], "ogA", to_x(3))
    arrived(og_buf.at[x ^ 3], "og3")
    send(og_buf.at[x ^ 3, 256:512], og_buf.at[x ^ 3, 256:512], "ogB", to_x(1))
    w_got = wblk.at[1 - q, :, w_mine]
    arrived(w_got, "w")
    send(w_got, w_got, "wf", to_seq(1))

    heads(lambda h: forward(2, h))

    arrived(kv3.at[s8 ^ 1], "kvo3")
    for m in (1, 3, 2):
        arrived(kv3.at[s8 ^ (2 * m + 1)], "kvf3_%d" % m)

    def last_level(h):
        forward(3, h)
        inverse = 1.0 / l_run[h]
        l_run[h] = inverse
        attended = (n_run[h] * inverse).astype(BF)
        attp[h] = attended
        att_buf[q, :, head_cols(h)] = dot(unperm[...], attended).astype(BF)
        block = att_buf.at[q, :, head_cols(h)]
        remote(block, block, "att0", to_y(y ^ 1), extra=h).start()

    heads(last_level)
    for h in range(HL):
        block = att_buf.at[q, :, h * DH : (h + 1) * DH]
        sent.append(remote(block, block, "att%d" % h, to_y(y ^ 1)))

    og_in.wait()
    w_in.wait()
    arrived(og_buf.at[x ^ 2, 0:256], "ogA")
    arrived(og_buf.at[x ^ 2, 256:512], "ogB")
    arrived(wblk.at[1 - q, :, w_other], "wf")

    def grad_part(which, dst):
        def tile(b):
            rows = pl.ds(pl.multiple_of(b * 256, 256), 256)
            total = dot_t(og_buf[0, rows, :], wblk[which, :, 0:512])
            for xx in range(1, 4):
                total += dot_t(og_buf[xx, rows, :], wblk[which, :, xx * 512 : (xx + 1) * 512])
            dst[rows, :] = total.astype(dst.dtype)

        loop(2, tile)

    grad_part(1 - q, g_send)
    send(g_send, g_recv, "g", to_y(y ^ 1))

    order = (2, 3, 1, 0)

    def transposed(hb, which):
        for h in range(HL):
            att_t[hb, h * DH : (h + 1) * DH, :] = dot_t(eye[:DH, :DH], att_buf[which, :, h * DH : (h + 1) * DH]).astype(BF)

    def weight_part(hb, i, cc):
        cols = pl.ds(pl.multiple_of(cc * 256, 256), 256)
        return dot(att_t[hb], og_buf[z ^ order[i], :, cols])

    def weight_first(hb):
        for i in range(4):
            gc_s[hb, i] = weight_part(hb, i, 1 - core).astype(BF)
            if i == 0:
                send(gc_s.at[hb, 0], gc_r.at[hb, 0], "gcA%d" % hb, to_seq(1))
        send(gc_s.at[hb, 1:4], gc_r.at[hb, 1:4], "gcB%d" % hb, to_seq(1))

    def weight_second(hb):
        arrived(gc_r.at[hb, 0], "gcA%d" % hb)
        gz_s[hb, 0] = (weight_part(hb, 0, core) + gc_r[hb, 0].astype(F32)).astype(BF)
        send(gz_s.at[hb, 0, 0:256], gz_a.at[hb], "za%d" % hb, to_seq(2))
        send(gz_s.at[hb, 0, 256:512], gz_b.at[hb], "zb%d" % hb, to_seq(6))
        arrived(gc_r.at[hb, 1:4], "gcB%d" % hb)
        for i in range(1, 4):
            gz_f[hb, i - 1] = weight_part(hb, i, core) + gc_r[hb, i].astype(F32)

    def weight_third(hb):
        arrived(gz_a.at[hb], "za%d" % hb)
        gz_s[hb, 1, 0:256, :] = (gz_f[hb, 0, 0:256, :] + gz_a[hb].astype(F32)).astype(BF)
        gz_s[hb, 1, 256:512, :] = gz_f[hb, 0, 256:512, :].astype(BF)
        send(gz_s.at[hb, 1], gz_r.at[hb, 1], "z3%d" % hb, to_seq(6))
        arrived(gz_b.at[hb], "zb%d" % hb)
        gz_s[hb, 2, 0:256, :] = gz_f[hb, 1, 0:256, :].astype(BF)
        gz_s[hb, 2, 256:512, :] = (gz_f[hb, 1, 256:512, :] + gz_b[hb].astype(F32)).astype(BF)
        send(gz_s.at[hb, 2], gz_r.at[hb, 0], "z1%d" % hb, to_seq(2))

    def last_hop(hb):
        i = ID["y0"]
        return pltpu.make_async_remote_copy(
            src_ref=gy_s.at[hb], dst_ref=gy_r.at[yh], send_sem=ss.at[i + hb], recv_sem=rs.at[i + yh],
            device_id=to_y(3 * q if hb == 0 else q + 1), device_id_type=pl.DeviceIdType.MESH,
        )

    def weight_fourth(hb):
        arrived(gz_r.at[hb, 0], "z1%d" % hb)
        arrived(gz_r.at[hb, 1], "z3%d" % hb)
        total = gz_f[hb, 2] + gz_r[hb, 0].astype(F32) + gz_r[hb, 1].astype(F32)
        gy_s[hb] = total.astype(BF)
        if hb == 1:
            last_hop(1).start()
            return

        @pl.when(yh == q)
        def _():
            gy_r[yh] = gy_s[0]

        @pl.when(yh != q)
        def _():
            last_hop(0).start()

    def result_part(i):
        cols = pl.ds(pl.multiple_of((x ^ order[i]) * 512, 512), 512)
        return dot(att_buf[0], wblk[0, :, cols]) + dot(att_buf[1], wblk[1, :, cols])

    transposed(0, q)
    weight_first(0)
    grad_part(q, g_own)
    weight_second(0)

    for h in range(HL):
        arrived(att_buf.at[1 - q, :, h * DH : (h + 1) * DH], "att%d" % h)
    res_s[0] = result_part(0).astype(BF)
    send(res_s.at[0, 0:256], res_a, "ra", to_x(1))
    send(res_s.at[0, 256:512], res_b, "rb", to_x(3))
    transposed(1, 1 - q)
    weight_first(1)
    for i in range(1, 4):
        res_f[i - 1] = result_part(i)
    weight_third(0)
    weight_second(1)
    arrived(res_a, "ra")
    res_s[1, 0:256, :] = (res_f[0, 0:256, :] + res_a[...].astype(F32)).astype(BF)
    res_s[1, 256:512, :] = res_f[0, 256:512, :].astype(BF)
    send(res_s.at[1], res_r.at[1], "r3", to_x(3))
    arrived(res_b, "rb")
    res_s[2, 0:256, :] = res_f[1, 0:256, :].astype(BF)
    res_s[2, 256:512, :] = (res_f[1, 256:512, :] + res_b[...].astype(F32)).astype(BF)
    send(res_s.at[2], res_r.at[0], "r1", to_x(1))
    weight_third(1)

    arrived(g_recv, "g")

    def grad_total(b):
        rows = pl.ds(pl.multiple_of(b * 256, 256), 256)
        stage[0, rows, :] = (g_own[rows, :] + g_recv[rows, :].astype(F32)).astype(BF)

    loop(2, grad_total)
    permuted(stage.at[0], gp)

    def backward(level, h):
        n = R >> level
        keys = keys_of(level, h, 0)
        vals = keys_of(level, h, 1)
        grads = chosen(gp[h].astype(F32), level, h)
        factor = jnp.exp2(mms[level][h] - chosen(m_run[h], level, h)) * chosen(l_run[h], level, h)
        scaled = grads * factor
        delta = jnp.sum(scaled * chosen(attp[h].astype(F32), level, h), axis=1, keepdims=True)
        scaled = scaled.astype(BF)
        e = es[level][h]
        ds = (e.astype(F32) * (dot_t(scaled, vals) - delta)).astype(BF)
        dq = dot(ds, keys) * SCALE
        if level == 0:
            dqa[h] += dq
        elif level == 3:
            dqa[h] = placed(dq, level, h, 0.0)
        else:
            dqa[h] += placed(dq, level, h, 0.0)
        scaled_t = dot_t(eye[:DH, :DH], scaled).astype(BF)
        query_t = dot_t(eye[:DH, :DH], chosen_bf(qp[h], level, h)).astype(BF)
        dv_t = dot(scaled_t, e)
        dk_t = dot(query_t, ds) * SCALE
        both = dot_t(eye[...], jnp.concatenate([dk_t, dv_t], axis=0).astype(BF))
        if level == 0:
            dk0[h] = both[:, :DH]
            dv0[h] = both[:, DH:]
        else:
            shape = snd[level].shape[:-1] + (DH,)
            snd[level][..., head_cols(h)] = both[:, :DH].astype(BF).reshape(shape)
            snd[level][..., head_cols(h + HL)] = both[:, DH:].astype(BF).reshape(shape)

    zb = z % 2
    heads(lambda h: backward(3, h))
    send(snd3.at[:, 1 - core], cr3, "c3", to_seq(1))
    heads(lambda h: backward(2, h))
    send(snd2.at[:, 1 - core], cr2, "c2", to_seq(1))
    arrived(cr3, "c3")
    for m in (2, 1, 3):
        zs3[m - 1] = (snd3[z ^ m, core].astype(F32) + cr3[z ^ m].astype(F32)).astype(BF)
        send(zs3.at[m - 1], rz3.at[m - 1], "b3_%d" % m, to_seq(2 * m))
    heads(lambda h: backward(1, h))
    send(snd1.at[1 - core], cr1, "c1", to_seq(1))
    arrived(cr2, "c2")
    zs2[...] = (snd2[zb ^ 1, core].astype(F32) + cr2[zb ^ 1].astype(F32)).astype(BF)
    send(zs2, rz2, "b2_1", to_seq(2))
    weight_fourth(0)
    heads(lambda h: backward(0, h))

    def natural(dst):
        def tile(b):
            rows = pl.ds(pl.multiple_of(b * 256, 256), 256)
            dst[rows, :] = dot(unperm[rows, :], back[...]).astype(BF)

        loop(2, tile)

    for h in range(HL):
        back[:, h * DH : (h + 1) * DH] = dqa[h].astype(BF)
    natural(dq_o)

    arrived(res_r.at[0], "r1")
    arrived(res_r.at[1], "r3")

    def result_total(b):
        rows = pl.ds(pl.multiple_of(b * 128, 128), 128)
        res_o[rows, :] = (res_f[2, rows, :] + res_r[0, rows, :].astype(F32) + res_r[1, rows, :].astype(F32)).astype(BF)

    loop(4, result_total)
    weight_fourth(1)

    arrived(cr1, "c1")
    for m in (1, 3, 2):
        arrived(rz3.at[m - 1], "b3_%d" % m)
    arrived(rz2, "b2_1")

    for which, start_grad, dst in ((0, dk0, dk_o), (1, dv0, dv_o)):

        def key_total(h, which=which, start_grad=start_grad):
            total = start_grad[h]
            cols = head_cols(h + HL * which)
            owed = snd1[core, :, cols].astype(F32) + cr1[:, cols].astype(F32)
            total += placed(owed, 1, h, 0.0)
            owed = snd2[zb, core, :, cols].astype(F32) + cr2[zb, :, cols].astype(F32) + rz2[:, cols].astype(F32)
            total += placed(owed, 2, h, 0.0)
            owed = snd3[z, core, :, cols].astype(F32) + cr3[z, :, cols].astype(F32)
            for m in range(3):
                owed += rz3[m, :, cols].astype(F32)
            total += placed(owed, 3, h, 0.0)
            back[:, head_cols(h)] = total.astype(BF)

        heads(key_total)
        natural(dst)

    for source in range(2):

        @pl.when(jnp.logical_not((yh == source) & (q == yh)))
        def _(source=source):
            arrived(gy_r.at[source], "y%d" % source)

    gw_o[...] = (gy_r[0].astype(F32) + gy_r[1].astype(F32)).astype(BF)

    last_hop(1).wait_send()

    @pl.when(yh != q)
    def _():
        last_hop(0).wait_send()

    for copy in sent:
        copy.wait_send()


def hand_over(*refs):
    sources, targets, held, sems = refs[:5], refs[5:10], refs[10:15], refs[15]
    reads = [pltpu.make_async_copy(sources[i], held[i], sems.at[0, i]) for i in range(5)]
    writes = [pltpu.make_async_copy(held[i], targets[i], sems.at[1, i]) for i in range(5)]
    for copy in reads:
        copy.start()
    for i in range(5):
        reads[i].wait()
        writes[i].start()
    for copy in writes:
        copy.wait()


def shards(queries, keys, values, offsets, out_weight, out_grad):
    wide = jax.ShapeDtypeStruct((R, C), BF)
    any_spec = pl.BlockSpec(memory_space=pl.ANY)
    vmem = pl.BlockSpec(memory_space=pltpu.VMEM)

    def bf(*shape):
        return pltpu.VMEM(shape, BF)

    def f32(*shape):
        return pltpu.VMEM(shape, F32)

    count = len(NAMES)
    outs = (wide, wide, wide, wide, jax.ShapeDtypeStruct((512, 256), BF))
    made = pl.pallas_call(
        kernel,
        out_shape=outs,
        in_specs=[pl.BlockSpec(memory_space=pltpu.SMEM)] + [any_spec] * 5,
        out_specs=[vmem] * 5,
        scratch_shapes=[
            bf(3, R, C), bf(R, R), bf(R, R), bf(R, R),
            bf(HL, R, DH), bf(HL, R, DH), bf(HL, R, DH),
            bf(2, 256, 1024), bf(4, 128, 1024), bf(8, 64, 1024),
            bf(HL, 512, R), bf(HL, 256, R), bf(HL, 128, R), bf(HL, 64, R),
            f32(HL, 512, DH), f32(HL, 256, DH), f32(HL, 128, DH), f32(HL, 64, DH),
            f32(HL, R, DH), f32(HL, R, DH), f32(HL, R, DH),
            bf(HL, R, DH), bf(2, R, C), bf(2, C, R),
            bf(4, R, C), bf(2, C, 2048),
            f32(R, C), bf(R, C), bf(R, C), bf(HL, R, DH),
            bf(3, R, C), bf(256, C), bf(256, C), bf(2, R, C), f32(3, R, C),
            bf(2, 4, C, 256), bf(2, 4, C, 256),
            bf(2, 3, C, 256), bf(2, 256, 256), bf(2, 256, 256), bf(2, 2, C, 256), f32(2, 3, C, 256),
            bf(2, 512, 256), bf(2, 512, 256),
            f32(HL, R, DH), f32(HL, R, DH), f32(HL, R, DH),
            bf(2, 256, 1024), bf(2, 2, 128, 1024), bf(4, 2, 64, 1024),
            bf(256, 1024), bf(2, 128, 1024), bf(4, 64, 1024),
            bf(128, 1024), bf(3, 64, 1024), bf(128, 1024), bf(3, 64, 1024),
            bf(R, C),
            pltpu.SemaphoreType.DMA((count,)), pltpu.SemaphoreType.DMA((count,)), pltpu.SemaphoreType.DMA((5,)),
        ],
        compiler_params=pltpu.CompilerParams(
            collective_id=0, has_side_effects=True, vmem_limit_bytes=60 * 1024 * 1024
        ),
    )(offsets, queries, keys, values, out_weight, out_grad)
    return pl.pallas_call(
        hand_over, out_shape=outs, in_specs=[any_spec] * 5, out_specs=[any_spec] * 5,
        scratch_shapes=[pltpu.VMEM(out.shape, BF) for out in outs] + [pltpu.SemaphoreType.DMA((2, 5))],
        compiler_params=pltpu.CompilerParams(vmem_limit_bytes=60 * 1024 * 1024),
    )(*made)


def solution(mesh):
    return jax.shard_map(
        shards,
        mesh=mesh,
        in_specs=(
            P("seq", "tp"),
            P("seq", "tp"),
            P("seq", "tp"),
            P(),
            P("tp", None),
            P("seq", "tp"),
        ),
        out_specs=(P("seq", "tp"), P("seq", "tp"), P("seq", "tp"), P("seq", "tp"), P("tp", "seq")),
        check_vma=False,
    )
```

```python
import jax
import jax.numpy as jnp
from jax import lax
from jax.experimental import pallas as pl
from jax.experimental.pallas import tpu as pltpu
from jax.sharding import PartitionSpec as P

DH = 128
LEV = 3
R = 512
C = 512
HL = 4
SCALE = DH**-0.5
K2E = SCALE * 1.4426950408889634
NEG = -1e30
BF = jnp.bfloat16
F32 = jnp.float32

NAMES = (
    ["og1a", "og1b", "og3a", "og3b", "ogA", "ogB", "w", "wf"]
    + ["kvo1", "kvo2", "kvo3", "kv2", "kvf2"]
    + ["kv3_1", "kv3_3", "kv3A", "kv3B", "kvf3_1", "kvf3_3", "kvf3_2"]
    + ["att0", "att1", "g0", "g1"]
    + ["ra", "rb", "r1a", "r1b", "r3a", "r3b"]
    + ["%s%d" % (name, hb) for hb in range(2) for name in ("gcA", "gcB", "za", "zb", "z1a", "z1b", "z3a", "z3b")]
    + ["y0", "y1"]
    + ["%s_%d" % (name, hp) for hp in range(2) for name in ("c1", "c2", "c3", "b2_1", "b3_1", "b3_2", "b3_3")]
)
ID = {name: i for i, name in enumerate(NAMES)}


def dot(a, b):
    return lax.dot_general(a, b, (((1,), (0,)), ((), ())), preferred_element_type=F32)


def dot_t(a, b):
    return lax.dot_general(a, b, (((1,), (1,)), ((), ())), preferred_element_type=F32)


def heads(body):
    for h in range(HL):
        body(h)


def loop(count, body):
    def step(i, carry):
        body(i)
        return carry

    lax.fori_loop(0, count, step, 0)


def kernel(
    offs, q_hbm, k_hbm, v_hbm, w_hbm, og_hbm,
    res_o, dq_o, dk_o, dv_o, gw_o,
    stage, perm, unperm, eye, qp, kp, vp, kv1, kv2, kv3, e0, e1, e2, e3, mm0, mm1, mm2, mm3,
    m_run, l_run, n_run, attp, att_buf, att_t, og_buf, wblk, g_own, g_send, g_recv, gp,
    res_s, res_a, res_b, res_r, res_f, gc_s, gc_r, gz_s, gz_a, gz_b, gz_r, gz_f, gz_t, gy_s, gy_r,
    dqa, dk0, dv0, snd1, snd2, snd3, cr1, cr2, cr3, zs2, zs3, rz2, rz3, back, qt0, qt1, qt2, qt3,
    ss, rs, ls,
):
    s = lax.axis_index("seq")
    t = lax.axis_index("tp")
    core = s % 2
    z = (s // 2) % 4
    yh = s // 8
    x = t % 4
    q = t // 4
    y = 2 * yh + q
    s_base = yh * 8
    s8 = s % 8
    kv = [None, kv1, kv2, kv3]
    es = [e0, e1, e2, e3]
    mms = [mm0, mm1, mm2, mm3]
    snd = [None, snd1, snd2, snd3]
    qts = [qt0, qt1, qt2, qt3]
    sent = {}

    def to_seq(mask):
        return (s_base + (s8 ^ mask), t)

    def to_x(mask):
        return (s, q * 4 + (x ^ mask))

    def to_y(yy):
        return ((yy // 2) * 8 + s8, (yy % 2) * 4 + x)

    def remote(src, dst, name, device, extra=0):
        i = ID[name] + extra
        return pltpu.make_async_remote_copy(
            src_ref=src, dst_ref=dst, send_sem=ss.at[i], recv_sem=rs.at[i],
            device_id=device, device_id_type=pl.DeviceIdType.MESH,
        )

    def send(src, dst, name, device):
        copy = remote(src, dst, name, device)
        copy.start()
        sent[name] = copy

    def left(name):
        sent.pop(name).wait_send()

    def arrived(dst, name):
        remote(dst, dst, name, to_seq(1)).wait_recv()

    def head_cols(h):
        return pl.ds(h * DH, DH)

    def local(src, dst, i):
        copy = pltpu.make_async_copy(src, dst, ls.at[i])
        copy.start()
        return copy

    barrier = pltpu.get_barrier_semaphore()
    peers = [to_seq(m) for m in range(1, 8)] + [to_x(1), to_x(3)] + [to_y((y + d) % 4) for d in (1, 2, 3)]
    for peer in peers:
        pl.semaphore_signal(barrier, inc=1, device_id=peer, device_id_type=pl.DeviceIdType.MESH)
    k_in = local(k_hbm, stage.at[0], 0)
    v_in = local(v_hbm, stage.at[1], 1)
    q_in = local(q_hbm, stage.at[2], 2)
    og_in = local(og_hbm, og_buf.at[x], 3)
    half = pl.ds(pl.multiple_of(q * 2048, 2048), 2048)
    w_in = local(w_hbm.at[:, half], wblk.at[q], 4)


    def place_of(i):
        return ((i & 1) << 8) | (((i >> 1) & 1) << 7) | (((i >> 2) & 1) << 6) | (i >> 3)

    rows_i = lax.broadcasted_iota(jnp.int32, (R, R), 0)
    cols_i = lax.broadcasted_iota(jnp.int32, (R, R), 1)
    perm[...] = jnp.where(rows_i == place_of(cols_i), 1.0, 0.0).astype(BF)

    def permuted(src, dst):
        def tile(b):
            rows = pl.ds(pl.multiple_of(b * 256, 256), 256)
            moved = dot(perm[rows, :], src[...]).astype(BF)
            for h in range(HL):
                dst[h, rows, :] = moved[:, h * DH : (h + 1) * DH]

        loop(2, tile)

    def phase_of(level, h):
        return offs[level - 1, t * HL + h]

    def chosen(value, level, h):
        for bit in range(level):
            n = value.shape[0] // 2
            flag = jnp.full((n, DH), (phase_of(level, h) >> bit) & 1, jnp.int32)
            value = jnp.where(flag == 1, value[n:], value[:n])
        return value

    def chosen_bf(value, level, h):
        return value if level == 0 else chosen(value.astype(F32), level, h).astype(BF)

    k_in.wait()
    permuted(stage.at[0], kp)
    v_in.wait()
    permuted(stage.at[1], vp)
    for level in (3, 2, 1):
        n = R >> level
        slot = s % (1 << level)

        def fill(h, level=level, n=n, slot=slot):
            kv[level][slot, :, head_cols(h)] = chosen_bf(kp[h], level, h)
            kv[level][slot, :, head_cols(h + HL)] = chosen_bf(vp[h], level, h)

        heads(fill)

    pl.semaphore_wait(barrier, len(peers))
    w_there = pl.ds(pl.multiple_of((1 - q) * 2048 + core * 1024, 1024), 1024)
    w_mine = pl.ds(pl.multiple_of(core * 1024, 1024), 1024)
    w_other = pl.ds(pl.multiple_of((1 - core) * 1024, 1024), 1024)

    def send_grads(name, rows, mask):
        send(og_hbm.at[rows : rows + 256], og_buf.at[x, rows : rows + 256], name, to_x(mask))

    mine = [kv[level].at[s % (1 << level)] if level else None for level in range(4)]
    send(mine[3], mine[3], "kv3_1", to_seq(2))
    send(mine[3], mine[3], "kv3_3", to_seq(6))
    send(mine[2], mine[2], "kv2", to_seq(2))
    send_grads("og1a", 0, 1)
    send_grads("og3b", 256, 3)
    send_grads("og1b", 256, 1)
    send_grads("og3a", 0, 3)
    send(w_hbm.at[:, w_there], wblk.at[q, :, w_mine], "w", to_y((y + 3 + 2 * core) % 4))
    for level in (1, 2, 3):
        send(mine[level], mine[level], "kvo%d" % level, to_seq(1))
    unperm[...] = jnp.where(cols_i == place_of(rows_i), 1.0, 0.0).astype(BF)
    eye[...] = jnp.where(rows_i == cols_i, 1.0, 0.0).astype(BF)
    q_in.wait()
    permuted(stage.at[2], qp)

    def placed(value, level, h, fill):
        phase = jnp.full(value.shape, phase_of(level, h), jnp.int32)
        order = [sum(((p >> (level - 1 - bit)) & 1) << bit for bit in range(level)) for p in range(1 << level)]
        return jnp.concatenate([jnp.where(phase == p, value, fill) for p in order], axis=0)

    def keys_of(level, h, which):
        if level == 0:
            return (kp, vp)[which][h]
        return kv[level][:, :, head_cols(h + HL * which)].reshape(R, DH)

    def forward(level, h):
        n = R >> level
        rows = min(n, 256)
        keys = keys_of(level, h, 0)
        vals = jnp.concatenate([keys_of(level, h, 1), jnp.ones((R, DH), BF)], axis=1)
        for b in range(0, n, rows):
            if level == 0:
                queries = qp[h, b : b + rows, :]
            else:
                queries = chosen_bf(qp[h], level, h)
            scores = dot_t(queries, keys) * K2E
            top = jnp.max(scores, axis=1, keepdims=True)
            e = jnp.exp2(scores - top).astype(BF)
            es[level][h, b : b + rows, :] = e
            nl = dot(e, vals)
            top = jnp.broadcast_to(top, (rows, DH))
            mms[level][h, b : b + rows, :] = top
            if level == 0:
                m_run[h, b : b + rows, :] = top
                n_run[h, b : b + rows, :] = nl[:, :DH]
                l_run[h, b : b + rows, :] = nl[:, DH:]
        if level > 0:
            old = m_run[h]
            this = placed(top, level, h, NEG)
            new = jnp.maximum(old, this)
            a_old = jnp.exp2(old - new)
            a_this = jnp.exp2(this - new)
            m_run[h] = new
            n_run[h] = n_run[h] * a_old + a_this * jnp.concatenate([nl[:, :DH]] * (1 << level), axis=0)
            l_run[h] = l_run[h] * a_old + a_this * jnp.concatenate([nl[:, DH:]] * (1 << level), axis=0)

    heads(lambda h: forward(0, h))

    arrived(kv1.at[core ^ 1], "kvo1")
    heads(lambda h: forward(1, h))

    s4 = s % 4
    for m, half_at in ((1, 0), (3, 1)):
        there = kv3.at[s8 ^ (2 * m)]
        arrived(there, "kv3_%d" % m)
        part = kv3.at[s8 ^ (2 * m), half_at * 32 : half_at * 32 + 32]
        send(part, part, ("kv3A", "kv3B")[half_at], to_seq(2 * (4 - m)))
        send(there, there, "kvf3_%d" % m, to_seq(1))
    arrived(og_buf.at[x ^ 1, 0:256], "og1a")
    send(og_buf.at[x ^ 1, 0:256], og_buf.at[x ^ 1, 0:256], "ogA", to_x(3))
    arrived(og_buf.at[x ^ 3, 256:512], "og3b")
    send(og_buf.at[x ^ 3, 256:512], og_buf.at[x ^ 3, 256:512], "ogB", to_x(1))
    there = kv2.at[s4 ^ 2]
    arrived(there, "kv2")
    send(there, there, "kvf2", to_seq(1))
    arrived(kv3.at[s8 ^ 4, 0:32], "kv3A")
    arrived(kv3.at[s8 ^ 4, 32:64], "kv3B")
    there = kv3.at[s8 ^ 4]
    send(there, there, "kvf3_2", to_seq(1))
    w_got = wblk.at[1 - q, :, w_mine]
    arrived(w_got, "w")
    send(w_got, w_got, "wf", to_seq(1))
    arrived(kv2.at[s4 ^ 1], "kvo2")
    arrived(kv2.at[s4 ^ 3], "kvf2")
    heads(lambda h: forward(2, h))
    arrived(kv3.at[s8 ^ 1], "kvo3")
    for m in (1, 3, 2):
        arrived(kv3.at[s8 ^ (2 * m + 1)], "kvf3_%d" % m)

    def last_level(h):
        forward(3, h)
        inverse = 1.0 / l_run[h]
        l_run[h] = inverse
        attended = (n_run[h] * inverse).astype(BF)
        attp[h] = attended
        att_buf[q, :, head_cols(h)] = dot(unperm[...], attended).astype(BF)

    heads(last_level)

    def send_attended(rh):
        block = att_buf.at[q, rh * 256 : (rh + 1) * 256]
        send(block, block, "att%d" % rh, to_y(y ^ 1))

    send_attended(0)
    send_attended(1)
    for level in range(4):
        for h in range(HL):
            mms[level][h] = jnp.exp2(mms[level][h] - chosen(m_run[h], level, h)) * chosen(l_run[h], level, h)
            qts[level][h] = dot_t(eye[:DH, :DH], chosen_bf(qp[h], level, h)).astype(BF)

    og_in.wait()
    w_in.wait()
    arrived(og_buf.at[x ^ 1, 256:512], "og1b")
    arrived(og_buf.at[x ^ 3, 0:256], "og3a")
    arrived(og_buf.at[x ^ 2, 0:256], "ogA")
    arrived(og_buf.at[x ^ 2, 256:512], "ogB")
    arrived(wblk.at[1 - q, :, w_other], "wf")

    def grad_part(which, dst, hp):
        feats = slice(hp * 256, hp * 256 + 256)
        total = dot_t(og_buf[0], wblk[which, feats, 0:512])
        for xx in range(1, 4):
            total += dot_t(og_buf[xx], wblk[which, feats, xx * 512 : (xx + 1) * 512])
        dst[hp] = total.astype(dst.dtype)

    def send_grad(hp):
        send(g_send.at[hp], g_recv.at[hp], "g%d" % hp, to_y(y ^ 1))

    grad_part(1 - q, g_send, 0)
    grad_part(1 - q, g_send, 1)

    order = (2, 3, 1, 0)

    def transposed(hb, which):
        for h in range(HL):
            att_t[hb, h * DH : (h + 1) * DH, :] = dot_t(eye[:DH, :DH], att_buf[which, :, h * DH : (h + 1) * DH]).astype(BF)

    def weight_part(hb, i, cc):
        cols = pl.ds(pl.multiple_of(cc * 256, 256), 256)
        return dot(att_t[hb], og_buf[z ^ order[i], :, cols])

    def weight_first(hb):
        for i in range(4):
            gc_s[hb, i] = weight_part(hb, i, 1 - core).astype(BF)
            if i == 0:
                send(gc_s.at[hb, 0], gc_r.at[hb, 0], "gcA%d" % hb, to_seq(1))
        send(gc_s.at[hb, 1:4], gc_r.at[hb, 1:4], "gcB%d" % hb, to_seq(1))

    def weight_second(hb):
        arrived(gc_r.at[hb, 0], "gcA%d" % hb)
        gz_s[hb, 0] = (weight_part(hb, 0, core) + gc_r[hb, 0].astype(F32)).astype(BF)
        send(gz_s.at[hb, 0, 0:256], gz_a.at[hb], "za%d" % hb, to_seq(2))
        send(gz_s.at[hb, 0, 256:512], gz_b.at[hb], "zb%d" % hb, to_seq(6))
        arrived(gc_r.at[hb, 1:4], "gcB%d" % hb)
        part = weight_part(hb, 1, core) + gc_r[hb, 1].astype(F32)
        gz_f[hb, 0] = part[0:256]
        gz_s[hb, 1, 256:512, :] = part[256:512].astype(BF)
        send(gz_s.at[hb, 1, 256:512], gz_r.at[hb, 1, 256:512], "z3b%d" % hb, to_seq(6))
        part = weight_part(hb, 2, core) + gc_r[hb, 2].astype(F32)
        gz_f[hb, 1] = part[256:512]
        gz_s[hb, 2, 0:256, :] = part[0:256].astype(BF)
        send(gz_s.at[hb, 2, 0:256], gz_r.at[hb, 0, 0:256], "z1a%d" % hb, to_seq(2))
        gz_t[hb] = weight_part(hb, 3, core) + gc_r[hb, 3].astype(F32)

    def weight_third(hb):
        arrived(gz_a.at[hb], "za%d" % hb)
        gz_s[hb, 1, 0:256, :] = (gz_f[hb, 0] + gz_a[hb].astype(F32)).astype(BF)
        send(gz_s.at[hb, 1, 0:256], gz_r.at[hb, 1, 0:256], "z3a%d" % hb, to_seq(6))
        arrived(gz_b.at[hb], "zb%d" % hb)
        gz_s[hb, 2, 256:512, :] = (gz_f[hb, 1] + gz_b[hb].astype(F32)).astype(BF)
        send(gz_s.at[hb, 2, 256:512], gz_r.at[hb, 0, 256:512], "z1b%d" % hb, to_seq(2))

    def last_hop(hb):
        i = ID["y0"]
        return pltpu.make_async_remote_copy(
            src_ref=gy_s.at[hb], dst_ref=gy_r.at[yh], send_sem=ss.at[i + hb], recv_sem=rs.at[i + yh],
            device_id=to_y(3 * q if hb == 0 else q + 1), device_id_type=pl.DeviceIdType.MESH,
        )

    def weight_fourth(hb):
        for rh, name in ((0, "z%da%d"), (1, "z%db%d")):
            arrived(gz_r.at[hb, 0, rh * 256 : rh * 256 + 256], name % (1, hb))
            arrived(gz_r.at[hb, 1, rh * 256 : rh * 256 + 256], name % (3, hb))
        total = gz_t[hb] + gz_r[hb, 0].astype(F32) + gz_r[hb, 1].astype(F32)
        gy_s[hb] = total.astype(BF)
        if hb == 1:
            last_hop(1).start()
            return

        @pl.when(yh == q)
        def _():
            gy_r[yh] = gy_s[0]

        @pl.when(yh != q)
        def _():
            last_hop(0).start()

    def result_part(i, rh):
        rows = slice(rh * 256, rh * 256 + 256)
        cols = pl.ds(pl.multiple_of((x ^ order[i]) * 512, 512), 512)
        return dot(att_buf[0, rows, :], wblk[0, :, cols]) + dot(att_buf[1, rows, :], wblk[1, :, cols])

    transposed(0, q)
    weight_first(0)
    grad_part(q, g_own, 0)
    grad_part(q, g_own, 1)
    weight_second(0)

    arrived(att_buf.at[1 - q, 0:256], "att0")
    res_s[0, 0:256, :] = result_part(0, 0).astype(BF)
    send(res_s.at[0, 0:256], res_a, "ra", to_x(1))
    res_s[2, 0:256, :] = result_part(2, 0).astype(BF)
    send(res_s.at[2, 0:256], res_r.at[0, 0:256], "r1a", to_x(1))
    res_f[0, 0:256, :] = result_part(1, 0)
    res_f[1, 0:256, :] = result_part(3, 0)
    left("att0")
    left("att1")
    send_grad(0)
    send_grad(1)

    def result_hand_on_a():
        arrived(res_a, "ra")
        res_s[1, 0:256, :] = (res_f[0, 0:256, :] + res_a[...].astype(F32)).astype(BF)
        send(res_s.at[1, 0:256], res_r.at[1, 0:256], "r3a", to_x(3))

    def result_hand_on_b():
        arrived(res_b, "rb")
        res_s[2, 256:512, :] = (res_f[0, 256:512, :] + res_b[...].astype(F32)).astype(BF)
        send(res_s.at[2, 256:512], res_r.at[0, 256:512], "r1b", to_x(1))

    def result_second():
        arrived(att_buf.at[1 - q, 256:512], "att1")
        transposed(1, 1 - q)
        weight_first(1)
        res_s[0, 256:512, :] = result_part(0, 1).astype(BF)
        send(res_s.at[0, 256:512], res_b, "rb", to_x(3))
        res_s[1, 256:512, :] = result_part(1, 1).astype(BF)
        send(res_s.at[1, 256:512], res_r.at[1, 256:512], "r3b", to_x(3))
        res_f[0, 256:512, :] = result_part(2, 1)
        result_hand_on_a()
        weight_third(0)
        weight_second(1)
        res_f[1, 256:512, :] = result_part(3, 1)
        result_hand_on_b()

    def grad_total(hp):
        arrived(g_recv.at[hp], "g%d" % hp)
        moved = dot(perm[...], (g_own[hp] + g_recv[hp].astype(F32)).astype(BF)).astype(BF)
        gp[2 * hp] = moved[:, :DH]
        gp[2 * hp + 1] = moved[:, DH:]

    def grad_cols(h, which):
        return pl.ds((h // 2) * 512 + which * 256 + (h % 2) * DH, DH)

    def backward(level, h):
        n = R >> level
        keys = keys_of(level, h, 0)
        vals = keys_of(level, h, 1)
        grads = chosen(gp[h].astype(F32), level, h)
        scaled = grads * mms[level][h]
        delta = jnp.sum(scaled * chosen(attp[h].astype(F32), level, h), axis=1, keepdims=True)
        scaled = scaled.astype(BF)
        e = es[level][h]
        ds = (e.astype(F32) * (dot_t(scaled, vals) - delta)).astype(BF)
        dq = dot(ds, keys) * SCALE
        if level == 0:
            dqa[h] += dq
        elif level == 3:
            dqa[h] = placed(dq, level, h, 0.0)
        else:
            dqa[h] += placed(dq, level, h, 0.0)
        scaled_t = dot_t(eye[:DH, :DH], scaled).astype(BF)
        dv_t = dot(scaled_t, e)
        dk_t = dot(qts[level][h], ds) * SCALE
        both = dot_t(eye[...], jnp.concatenate([dk_t, dv_t], axis=0).astype(BF))
        if level == 0:
            dk0[h] = both[:, :DH]
            dv0[h] = both[:, DH:]
        else:
            shape = snd[level].shape[:-1] + (DH,)
            snd[level][..., grad_cols(h, 0)] = both[:, :DH].astype(BF).reshape(shape)
            snd[level][..., grad_cols(h, 1)] = both[:, DH:].astype(BF).reshape(shape)

    zb = z % 2

    def pair(level, hp):
        backward(level, 2 * hp)
        backward(level, 2 * hp + 1)

    def owed_core(level, hp):
        cols = slice(hp * 512, hp * 512 + 512)
        if level == 3:
            send(snd3.at[:, 1 - core, :, cols], cr3.at[:, :, cols], "c3_%d" % hp, to_seq(1))
        elif level == 2:
            send(snd2.at[:, 1 - core, :, cols], cr2.at[:, :, cols], "c2_%d" % hp, to_seq(1))
        else:
            send(snd1.at[1 - core, :, cols], cr1.at[:, cols], "c1_%d" % hp, to_seq(1))

    def owed_z(level, hp):
        cols = slice(hp * 512, hp * 512 + 512)
        if level == 3:
            arrived(cr3.at[:, :, cols], "c3_%d" % hp)
            for m in (2, 1, 3):
                zs3[m - 1, :, cols] = (snd3[z ^ m, core, :, cols].astype(F32) + cr3[z ^ m, :, cols].astype(F32)).astype(BF)
                send(zs3.at[m - 1, :, cols], rz3.at[m - 1, :, cols], "b3_%d_%d" % (m, hp), to_seq(2 * m))
        else:
            arrived(cr2.at[:, :, cols], "c2_%d" % hp)
            zs2[:, cols] = (snd2[zb ^ 1, core, :, cols].astype(F32) + cr2[zb ^ 1, :, cols].astype(F32)).astype(BF)
            send(zs2.at[:, cols], rz2.at[:, cols], "b2_1_%d" % hp, to_seq(2))

    result_second()
    grad_total(0)
    pair(3, 0)
    owed_core(3, 0)
    weight_third(1)
    pair(2, 0)
    owed_core(2, 0)
    owed_z(3, 0)
    pair(1, 0)
    owed_core(1, 0)
    owed_z(2, 0)
    pair(0, 0)
    weight_fourth(0)
    grad_total(1)
    pair(3, 1)
    owed_core(3, 1)
    pair(2, 1)
    owed_core(2, 1)
    owed_z(3, 1)
    pair(1, 1)
    owed_core(1, 1)
    owed_z(2, 1)
    weight_fourth(1)
    pair(0, 1)

    def natural(dst, hp):
        cols = slice(hp * 256, hp * 256 + 256)
        dst[:, cols] = dot(unperm[...], back[:, cols]).astype(BF)

    def key_total(hp):
        cols_in = slice(hp * 512, hp * 512 + 512)
        arrived(cr1.at[:, cols_in], "c1_%d" % hp)
        arrived(rz2.at[:, cols_in], "b2_1_%d" % hp)
        for m in (1, 3, 2):
            arrived(rz3.at[m - 1, :, cols_in], "b3_%d_%d" % (m, hp))
        for which, start_grad, dst in ((0, dk0, dk_o), (1, dv0, dv_o)):
            for h in (2 * hp, 2 * hp + 1):
                total = start_grad[h]
                cols = grad_cols(h, which)
                owed = snd1[core, :, cols].astype(F32) + cr1[:, cols].astype(F32)
                total += placed(owed, 1, h, 0.0)
                owed = snd2[zb, core, :, cols].astype(F32) + cr2[zb, :, cols].astype(F32) + rz2[:, cols].astype(F32)
                total += placed(owed, 2, h, 0.0)
                owed = snd3[z, core, :, cols].astype(F32) + cr3[z, :, cols].astype(F32)
                for m in range(3):
                    owed += rz3[m, :, cols].astype(F32)
                total += placed(owed, 3, h, 0.0)
                back[:, h * DH : (h + 1) * DH] = total.astype(BF)
            natural(dst, hp)

    key_total(0)
    for h in range(HL):
        back[:, h * DH : (h + 1) * DH] = dqa[h].astype(BF)
    natural(dq_o, 0)
    natural(dq_o, 1)

    for rh, name in ((0, "r%da"), (1, "r%db")):
        arrived(res_r.at[0, rh * 256 : rh * 256 + 256], name % 1)
        arrived(res_r.at[1, rh * 256 : rh * 256 + 256], name % 3)

    def result_total(b):
        rows = pl.ds(pl.multiple_of(b * 128, 128), 128)
        res_o[rows, :] = (res_f[1, rows, :] + res_r[0, rows, :].astype(F32) + res_r[1, rows, :].astype(F32)).astype(BF)

    loop(4, result_total)
    key_total(1)

    for source in range(2):

        @pl.when(jnp.logical_not((yh == source) & (q == yh)))
        def _(source=source):
            arrived(gy_r.at[source], "y%d" % source)

    gw_o[...] = (gy_r[0].astype(F32) + gy_r[1].astype(F32)).astype(BF)

    last_hop(1).wait_send()

    @pl.when(yh != q)
    def _():
        last_hop(0).wait_send()

    for copy in sent.values():
        copy.wait_send()


def hand_over(*refs):
    sources, targets, held, sems = refs[:5], refs[5:10], refs[10:15], refs[15]
    reads = [pltpu.make_async_copy(sources[i], held[i], sems.at[0, i]) for i in range(5)]
    writes = [pltpu.make_async_copy(held[i], targets[i], sems.at[1, i]) for i in range(5)]
    for copy in reads:
        copy.start()
    for i in range(5):
        reads[i].wait()
        writes[i].start()
    for copy in writes:
        copy.wait()


def shards(queries, keys, values, offsets, out_weight, out_grad):
    wide = jax.ShapeDtypeStruct((R, C), BF)
    any_spec = pl.BlockSpec(memory_space=pl.ANY)
    vmem = pl.BlockSpec(memory_space=pltpu.VMEM)

    def bf(*shape):
        return pltpu.VMEM(shape, BF)

    def f32(*shape):
        return pltpu.VMEM(shape, F32)

    count = len(NAMES)
    outs = (wide, wide, wide, wide, jax.ShapeDtypeStruct((512, 256), BF))
    made = pl.pallas_call(
        kernel,
        out_shape=outs,
        in_specs=[pl.BlockSpec(memory_space=pltpu.SMEM)] + [any_spec] * 5,
        out_specs=[vmem] * 5,
        scratch_shapes=[
            bf(3, R, C), bf(R, R), bf(R, R), bf(R, R),
            bf(HL, R, DH), bf(HL, R, DH), bf(HL, R, DH),
            bf(2, 256, 1024), bf(4, 128, 1024), bf(8, 64, 1024),
            bf(HL, 512, R), bf(HL, 256, R), bf(HL, 128, R), bf(HL, 64, R),
            f32(HL, 512, DH), f32(HL, 256, DH), f32(HL, 128, DH), f32(HL, 64, DH),
            f32(HL, R, DH), f32(HL, R, DH), f32(HL, R, DH),
            bf(HL, R, DH), bf(2, R, C), bf(2, C, R),
            bf(4, R, C), bf(2, C, 2048),
            f32(2, R, 256), bf(2, R, 256), bf(2, R, 256), bf(HL, R, DH),
            bf(3, R, C), bf(256, C), bf(256, C), bf(2, R, C), f32(2, R, C),
            bf(2, 4, C, 256), bf(2, 4, C, 256),
            bf(2, 3, C, 256), bf(2, 256, 256), bf(2, 256, 256), bf(2, 2, C, 256), f32(2, 2, 256, 256), f32(2, C, 256),
            bf(2, 512, 256), bf(2, 512, 256),
            f32(HL, R, DH), f32(HL, R, DH), f32(HL, R, DH),
            bf(2, 256, 1024), bf(2, 2, 128, 1024), bf(4, 2, 64, 1024),
            bf(256, 1024), bf(2, 128, 1024), bf(4, 64, 1024),
            bf(128, 1024), bf(3, 64, 1024), bf(128, 1024), bf(3, 64, 1024),
            bf(R, C),
            bf(HL, DH, 512), bf(HL, DH, 256), bf(HL, DH, 128), bf(HL, DH, 64),
            pltpu.SemaphoreType.DMA((count,)), pltpu.SemaphoreType.DMA((count,)), pltpu.SemaphoreType.DMA((5,)),
        ],
        compiler_params=pltpu.CompilerParams(
            collective_id=0, has_side_effects=True, vmem_limit_bytes=60 * 1024 * 1024
        ),
    )(offsets, queries, keys, values, out_weight, out_grad)
    return pl.pallas_call(
        hand_over, out_shape=outs, in_specs=[any_spec] * 5, out_specs=[any_spec] * 5,
        scratch_shapes=[pltpu.VMEM(out.shape, BF) for out in outs] + [pltpu.SemaphoreType.DMA((2, 5))],
        compiler_params=pltpu.CompilerParams(vmem_limit_bytes=60 * 1024 * 1024),
    )(*made)


def solution(mesh):
    return jax.shard_map(
        shards,
        mesh=mesh,
        in_specs=(
            P("seq", "tp"),
            P("seq", "tp"),
            P("seq", "tp"),
            P(),
            P("tp", None),
            P("seq", "tp"),
        ),
        out_specs=(P("seq", "tp"), P("seq", "tp"), P("seq", "tp"), P("seq", "tp"), P("tp", "seq")),
        check_vma=False,
    )
```

```python
import jax
import jax.numpy as jnp
from jax import lax
from jax.experimental import pallas as pl
from jax.experimental.pallas import tpu as pltpu
from jax.sharding import PartitionSpec as P

DH = 128
LEV = 3
R = 512
C = 512
HL = 4
SCALE = DH**-0.5
K2E = SCALE * 1.4426950408889634
NEG = -1e30
BF = jnp.bfloat16
F32 = jnp.float32

NAMES = (
    ["og1a", "og1b", "og3a", "og3b", "ogA", "ogB", "w", "wf"]
    + ["kvo1", "kvo2", "kvo3", "kv2", "kvf2"]
    + ["kv3_1", "kv3_3", "kv3A", "kv3B", "kvf3_1", "kvf3_3", "kvf3_2"]
    + ["att0", "att1", "g0", "g1"]
    + ["ra", "rb", "r1a", "r1b", "r3a", "r3b"]
    + ["%s%d" % (name, hb) for hb in range(2) for name in ("gcA", "gcB", "za", "zb", "z1a", "z1b", "z3a", "z3b")]
    + ["y0", "y1"]
    + ["%s_%d" % (name, hp) for hp in range(2) for name in ("c1", "c2", "c3", "b2_1", "b3_1", "b3_2", "b3_3")]
)
ID = {name: i for i, name in enumerate(NAMES)}


def dot(a, b):
    return lax.dot_general(a, b, (((1,), (0,)), ((), ())), preferred_element_type=F32)


def dot_t(a, b):
    return lax.dot_general(a, b, (((1,), (1,)), ((), ())), preferred_element_type=F32)


def heads(body):
    for h in range(HL):
        body(h)


def loop(count, body):
    def step(i, carry):
        body(i)
        return carry

    lax.fori_loop(0, count, step, 0)


def kernel(
    offs, q_hbm, k_hbm, v_hbm, w_hbm, og_hbm,
    res_out, dq_out, dk_out, dv_out, gw_out,
    res_o, dq_o, dk_o, dv_o, gw_o,
    stage, perm, unperm, eye, qp, kp, vp, kv1, kv2, kv3, e0, e1, e2, e3, mm0, mm1, mm2, mm3,
    m_run, l_run, n_run, attp, att_buf, att_t, og_buf, wblk, g_own, g_send, g_recv, gp,
    res_s, res_a, res_b, res_r, res_f, gc_s, gc_r, gz_s, gz_a, gz_b, gz_r, gz_f, gz_t, gy_s, gy_r,
    dqa, dk0, dv0, snd1, snd2, snd3, cr1, cr2, cr3, zs2, zs3, rz2, rz3, back, qt0, qt1, qt2, qt3,
    ss, rs, ls,
):
    s = lax.axis_index("seq")
    t = lax.axis_index("tp")
    core = s % 2
    z = (s // 2) % 4
    yh = s // 8
    x = t % 4
    q = t // 4
    y = 2 * yh + q
    s_base = yh * 8
    s8 = s % 8
    kv = [None, kv1, kv2, kv3]
    es = [e0, e1, e2, e3]
    mms = [mm0, mm1, mm2, mm3]
    snd = [None, snd1, snd2, snd3]
    qts = [qt0, qt1, qt2, qt3]
    sent = {}

    def to_seq(mask):
        return (s_base + (s8 ^ mask), t)

    def to_x(mask):
        return (s, q * 4 + (x ^ mask))

    def to_y(yy):
        return ((yy // 2) * 8 + s8, (yy % 2) * 4 + x)

    def remote(src, dst, name, device, extra=0):
        i = ID[name] + extra
        return pltpu.make_async_remote_copy(
            src_ref=src, dst_ref=dst, send_sem=ss.at[i], recv_sem=rs.at[i],
            device_id=device, device_id_type=pl.DeviceIdType.MESH,
        )

    def send(src, dst, name, device):
        copy = remote(src, dst, name, device)
        copy.start()
        sent[name] = copy

    def left(name):
        sent.pop(name).wait_send()

    def arrived(dst, name):
        remote(dst, dst, name, to_seq(1)).wait_recv()

    def head_cols(h):
        return pl.ds(h * DH, DH)

    def local(src, dst, i):
        copy = pltpu.make_async_copy(src, dst, ls.at[i])
        copy.start()
        return copy

    barrier = pltpu.get_barrier_semaphore()
    peers = [to_seq(m) for m in range(1, 8)] + [to_x(1), to_x(3)] + [to_y((y + d) % 4) for d in (1, 2, 3)]
    for peer in peers:
        pl.semaphore_signal(barrier, inc=1, device_id=peer, device_id_type=pl.DeviceIdType.MESH)
    k_in = local(k_hbm, stage.at[0], 0)
    v_in = local(v_hbm, stage.at[1], 1)
    q_in = local(q_hbm, stage.at[2], 2)
    og_in = local(og_hbm, og_buf.at[x], 3)
    half = pl.ds(pl.multiple_of(q * 2048, 2048), 2048)
    w_in = local(w_hbm.at[:, half], wblk.at[q], 4)


    def place_of(i):
        return ((i & 1) << 8) | (((i >> 1) & 1) << 7) | (((i >> 2) & 1) << 6) | (i >> 3)

    rows_i = lax.broadcasted_iota(jnp.int32, (R, R), 0)
    cols_i = lax.broadcasted_iota(jnp.int32, (R, R), 1)
    perm[...] = jnp.where(rows_i == place_of(cols_i), 1.0, 0.0).astype(BF)

    def permuted(src, dst):
        def tile(b):
            rows = pl.ds(pl.multiple_of(b * 256, 256), 256)
            moved = dot(perm[rows, :], src[...]).astype(BF)
            for h in range(HL):
                dst[h, rows, :] = moved[:, h * DH : (h + 1) * DH]

        loop(2, tile)

    def phase_of(level, h):
        return offs[level - 1, t * HL + h]

    def chosen(value, level, h):
        for bit in range(level):
            n = value.shape[0] // 2
            flag = jnp.full((n, DH), (phase_of(level, h) >> bit) & 1, jnp.int32)
            value = jnp.where(flag == 1, value[n:], value[:n])
        return value

    def chosen_bf(value, level, h):
        return value if level == 0 else chosen(value.astype(F32), level, h).astype(BF)

    k_in.wait()
    permuted(stage.at[0], kp)
    v_in.wait()
    permuted(stage.at[1], vp)
    for level in (3, 2, 1):
        n = R >> level
        slot = s % (1 << level)

        def fill(h, level=level, n=n, slot=slot):
            kv[level][slot, :, head_cols(h)] = chosen_bf(kp[h], level, h)
            kv[level][slot, :, head_cols(h + HL)] = chosen_bf(vp[h], level, h)

        heads(fill)

    pl.semaphore_wait(barrier, len(peers))
    w_there = pl.ds(pl.multiple_of((1 - q) * 2048 + core * 1024, 1024), 1024)
    w_mine = pl.ds(pl.multiple_of(core * 1024, 1024), 1024)
    w_other = pl.ds(pl.multiple_of((1 - core) * 1024, 1024), 1024)

    def send_grads(name, rows, mask):
        send(og_hbm.at[rows : rows + 256], og_buf.at[x, rows : rows + 256], name, to_x(mask))

    mine = [kv[level].at[s % (1 << level)] if level else None for level in range(4)]
    send(mine[3], mine[3], "kv3_1", to_seq(2))
    send(mine[3], mine[3], "kv3_3", to_seq(6))
    send(mine[2], mine[2], "kv2", to_seq(2))
    send_grads("og1a", 0, 1)
    send_grads("og3b", 256, 3)
    send_grads("og1b", 256, 1)
    send_grads("og3a", 0, 3)
    send(w_hbm.at[:, w_there], wblk.at[q, :, w_mine], "w", to_y((y + 3 + 2 * core) % 4))
    for level in (1, 2, 3):
        send(mine[level], mine[level], "kvo%d" % level, to_seq(1))
    unperm[...] = jnp.where(cols_i == place_of(rows_i), 1.0, 0.0).astype(BF)
    eye[...] = jnp.where(rows_i == cols_i, 1.0, 0.0).astype(BF)
    q_in.wait()
    permuted(stage.at[2], qp)

    def placed(value, level, h, fill):
        phase = jnp.full(value.shape, phase_of(level, h), jnp.int32)
        order = [sum(((p >> (level - 1 - bit)) & 1) << bit for bit in range(level)) for p in range(1 << level)]
        return jnp.concatenate([jnp.where(phase == p, value, fill) for p in order], axis=0)

    def keys_of(level, h, which):
        if level == 0:
            return (kp, vp)[which][h]
        return kv[level][:, :, head_cols(h + HL * which)].reshape(R, DH)

    def forward(level, h):
        n = R >> level
        rows = min(n, 256)
        keys = keys_of(level, h, 0)
        vals = jnp.concatenate([keys_of(level, h, 1), jnp.ones((R, DH), BF)], axis=1)
        for b in range(0, n, rows):
            if level == 0:
                queries = qp[h, b : b + rows, :]
            else:
                queries = chosen_bf(qp[h], level, h)
            scores = dot_t(queries, keys) * K2E
            top = jnp.max(scores, axis=1, keepdims=True)
            e = jnp.exp2(scores - top).astype(BF)
            es[level][h, b : b + rows, :] = e
            nl = dot(e, vals)
            top = jnp.broadcast_to(top, (rows, DH))
            mms[level][h, b : b + rows, :] = top
            if level == 0:
                m_run[h, b : b + rows, :] = top
                n_run[h, b : b + rows, :] = nl[:, :DH]
                l_run[h, b : b + rows, :] = nl[:, DH:]
        if level > 0:
            old = m_run[h]
            this = placed(top, level, h, NEG)
            new = jnp.maximum(old, this)
            a_old = jnp.exp2(old - new)
            a_this = jnp.exp2(this - new)
            m_run[h] = new
            n_run[h] = n_run[h] * a_old + a_this * jnp.concatenate([nl[:, :DH]] * (1 << level), axis=0)
            l_run[h] = l_run[h] * a_old + a_this * jnp.concatenate([nl[:, DH:]] * (1 << level), axis=0)

    heads(lambda h: forward(0, h))

    arrived(kv1.at[core ^ 1], "kvo1")
    heads(lambda h: forward(1, h))

    s4 = s % 4
    for m, half_at in ((1, 0), (3, 1)):
        there = kv3.at[s8 ^ (2 * m)]
        arrived(there, "kv3_%d" % m)
        part = kv3.at[s8 ^ (2 * m), half_at * 32 : half_at * 32 + 32]
        send(part, part, ("kv3A", "kv3B")[half_at], to_seq(2 * (4 - m)))
        send(there, there, "kvf3_%d" % m, to_seq(1))
    arrived(og_buf.at[x ^ 1, 0:256], "og1a")
    send(og_buf.at[x ^ 1, 0:256], og_buf.at[x ^ 1, 0:256], "ogA", to_x(3))
    arrived(og_buf.at[x ^ 3, 256:512], "og3b")
    send(og_buf.at[x ^ 3, 256:512], og_buf.at[x ^ 3, 256:512], "ogB", to_x(1))
    there = kv2.at[s4 ^ 2]
    arrived(there, "kv2")
    send(there, there, "kvf2", to_seq(1))
    arrived(kv3.at[s8 ^ 4, 0:32], "kv3A")
    arrived(kv3.at[s8 ^ 4, 32:64], "kv3B")
    there = kv3.at[s8 ^ 4]
    send(there, there, "kvf3_2", to_seq(1))
    w_got = wblk.at[1 - q, :, w_mine]
    arrived(w_got, "w")
    send(w_got, w_got, "wf", to_seq(1))
    arrived(kv2.at[s4 ^ 1], "kvo2")
    arrived(kv2.at[s4 ^ 3], "kvf2")
    heads(lambda h: forward(2, h))
    arrived(kv3.at[s8 ^ 1], "kvo3")
    for m in (1, 3, 2):
        arrived(kv3.at[s8 ^ (2 * m + 1)], "kvf3_%d" % m)

    def last_level(h):
        forward(3, h)
        inverse = 1.0 / l_run[h]
        l_run[h] = inverse
        attended = (n_run[h] * inverse).astype(BF)
        attp[h] = attended
        att_buf[q, :, head_cols(h)] = dot(unperm[...], attended).astype(BF)

    heads(last_level)

    def send_attended(rh):
        block = att_buf.at[q, rh * 256 : (rh + 1) * 256]
        send(block, block, "att%d" % rh, to_y(y ^ 1))

    send_attended(0)
    send_attended(1)
    for level in range(4):
        for h in range(HL):
            mms[level][h] = jnp.exp2(mms[level][h] - chosen(m_run[h], level, h)) * chosen(l_run[h], level, h)
            qts[level][h] = dot_t(eye[:DH, :DH], chosen_bf(qp[h], level, h)).astype(BF)

    og_in.wait()
    w_in.wait()
    arrived(og_buf.at[x ^ 1, 256:512], "og1b")
    arrived(og_buf.at[x ^ 3, 0:256], "og3a")
    arrived(og_buf.at[x ^ 2, 0:256], "ogA")
    arrived(og_buf.at[x ^ 2, 256:512], "ogB")
    arrived(wblk.at[1 - q, :, w_other], "wf")

    def grad_part(which, dst, hp):
        feats = slice(hp * 256, hp * 256 + 256)
        total = dot_t(og_buf[0], wblk[which, feats, 0:512])
        for xx in range(1, 4):
            total += dot_t(og_buf[xx], wblk[which, feats, xx * 512 : (xx + 1) * 512])
        dst[hp] = total.astype(dst.dtype)

    def send_grad(hp):
        send(g_send.at[hp], g_recv.at[hp], "g%d" % hp, to_y(y ^ 1))

    grad_part(1 - q, g_send, 0)
    grad_part(1 - q, g_send, 1)

    order = (2, 3, 1, 0)

    def transposed(hb, which):
        for h in range(HL):
            att_t[hb, h * DH : (h + 1) * DH, :] = dot_t(eye[:DH, :DH], att_buf[which, :, h * DH : (h + 1) * DH]).astype(BF)

    def weight_part(hb, i, cc):
        cols = pl.ds(pl.multiple_of(cc * 256, 256), 256)
        return dot(att_t[hb], og_buf[z ^ order[i], :, cols])

    def weight_first(hb):
        for i in range(4):
            gc_s[hb, i] = weight_part(hb, i, 1 - core).astype(BF)
            if i == 0:
                send(gc_s.at[hb, 0], gc_r.at[hb, 0], "gcA%d" % hb, to_seq(1))
        send(gc_s.at[hb, 1:4], gc_r.at[hb, 1:4], "gcB%d" % hb, to_seq(1))

    def weight_second(hb):
        arrived(gc_r.at[hb, 0], "gcA%d" % hb)
        gz_s[hb, 0] = (weight_part(hb, 0, core) + gc_r[hb, 0].astype(F32)).astype(BF)
        send(gz_s.at[hb, 0, 0:256], gz_a.at[hb], "za%d" % hb, to_seq(2))
        send(gz_s.at[hb, 0, 256:512], gz_b.at[hb], "zb%d" % hb, to_seq(6))
        arrived(gc_r.at[hb, 1:4], "gcB%d" % hb)
        part = weight_part(hb, 1, core) + gc_r[hb, 1].astype(F32)
        gz_f[hb, 0] = part[0:256]
        gz_s[hb, 1, 256:512, :] = part[256:512].astype(BF)
        send(gz_s.at[hb, 1, 256:512], gz_r.at[hb, 1, 256:512], "z3b%d" % hb, to_seq(6))
        part = weight_part(hb, 2, core) + gc_r[hb, 2].astype(F32)
        gz_f[hb, 1] = part[256:512]
        gz_s[hb, 2, 0:256, :] = part[0:256].astype(BF)
        send(gz_s.at[hb, 2, 0:256], gz_r.at[hb, 0, 0:256], "z1a%d" % hb, to_seq(2))
        gz_t[hb] = weight_part(hb, 3, core) + gc_r[hb, 3].astype(F32)

    def weight_third(hb):
        arrived(gz_a.at[hb], "za%d" % hb)
        gz_s[hb, 1, 0:256, :] = (gz_f[hb, 0] + gz_a[hb].astype(F32)).astype(BF)
        send(gz_s.at[hb, 1, 0:256], gz_r.at[hb, 1, 0:256], "z3a%d" % hb, to_seq(6))
        arrived(gz_b.at[hb], "zb%d" % hb)
        gz_s[hb, 2, 256:512, :] = (gz_f[hb, 1] + gz_b[hb].astype(F32)).astype(BF)
        send(gz_s.at[hb, 2, 256:512], gz_r.at[hb, 0, 256:512], "z1b%d" % hb, to_seq(2))

    def last_hop(hb):
        i = ID["y0"]
        return pltpu.make_async_remote_copy(
            src_ref=gy_s.at[hb], dst_ref=gy_r.at[yh], send_sem=ss.at[i + hb], recv_sem=rs.at[i + yh],
            device_id=to_y(3 * q if hb == 0 else q + 1), device_id_type=pl.DeviceIdType.MESH,
        )

    def weight_fourth(hb):
        for rh, name in ((0, "z%da%d"), (1, "z%db%d")):
            arrived(gz_r.at[hb, 0, rh * 256 : rh * 256 + 256], name % (1, hb))
            arrived(gz_r.at[hb, 1, rh * 256 : rh * 256 + 256], name % (3, hb))
        total = gz_t[hb] + gz_r[hb, 0].astype(F32) + gz_r[hb, 1].astype(F32)
        gy_s[hb] = total.astype(BF)
        if hb == 1:
            last_hop(1).start()
            return

        @pl.when(yh == q)
        def _():
            gy_r[yh] = gy_s[0]

        @pl.when(yh != q)
        def _():
            last_hop(0).start()

    def result_part(i, rh):
        rows = slice(rh * 256, rh * 256 + 256)
        cols = pl.ds(pl.multiple_of((x ^ order[i]) * 512, 512), 512)
        return dot(att_buf[0, rows, :], wblk[0, :, cols]) + dot(att_buf[1, rows, :], wblk[1, :, cols])

    transposed(0, q)
    weight_first(0)
    grad_part(q, g_own, 0)
    grad_part(q, g_own, 1)
    weight_second(0)

    arrived(att_buf.at[1 - q, 0:256], "att0")
    res_s[0, 0:256, :] = result_part(0, 0).astype(BF)
    send(res_s.at[0, 0:256], res_a, "ra", to_x(1))
    res_s[2, 0:256, :] = result_part(2, 0).astype(BF)
    send(res_s.at[2, 0:256], res_r.at[0, 0:256], "r1a", to_x(1))
    res_f[0, 0:256, :] = result_part(1, 0)
    res_f[1, 0:256, :] = result_part(3, 0)
    left("att0")
    left("att1")
    send_grad(0)
    send_grad(1)

    def result_hand_on_a():
        arrived(res_a, "ra")
        res_s[1, 0:256, :] = (res_f[0, 0:256, :] + res_a[...].astype(F32)).astype(BF)
        send(res_s.at[1, 0:256], res_r.at[1, 0:256], "r3a", to_x(3))

    def result_hand_on_b():
        arrived(res_b, "rb")
        res_s[2, 256:512, :] = (res_f[0, 256:512, :] + res_b[...].astype(F32)).astype(BF)
        send(res_s.at[2, 256:512], res_r.at[0, 256:512], "r1b", to_x(1))

    def result_second():
        arrived(att_buf.at[1 - q, 256:512], "att1")
        transposed(1, 1 - q)
        weight_first(1)
        res_s[0, 256:512, :] = result_part(0, 1).astype(BF)
        send(res_s.at[0, 256:512], res_b, "rb", to_x(3))
        res_s[1, 256:512, :] = result_part(1, 1).astype(BF)
        send(res_s.at[1, 256:512], res_r.at[1, 256:512], "r3b", to_x(3))
        res_f[0, 256:512, :] = result_part(2, 1)
        result_hand_on_a()
        weight_third(0)
        weight_second(1)
        res_f[1, 256:512, :] = result_part(3, 1)
        result_hand_on_b()

    def grad_total(hp):
        arrived(g_recv.at[hp], "g%d" % hp)
        moved = dot(perm[...], (g_own[hp] + g_recv[hp].astype(F32)).astype(BF)).astype(BF)
        gp[2 * hp] = moved[:, :DH]
        gp[2 * hp + 1] = moved[:, DH:]

    def grad_cols(h, which):
        return pl.ds((h // 2) * 512 + which * 256 + (h % 2) * DH, DH)

    def backward(level, h):
        n = R >> level
        keys = keys_of(level, h, 0)
        vals = keys_of(level, h, 1)
        grads = chosen(gp[h].astype(F32), level, h)
        scaled = grads * mms[level][h]
        delta = jnp.sum(scaled * chosen(attp[h].astype(F32), level, h), axis=1, keepdims=True)
        scaled = scaled.astype(BF)
        e = es[level][h]
        ds = (e.astype(F32) * (dot_t(scaled, vals) - delta)).astype(BF)
        dq = dot(ds, keys) * SCALE
        if level == 0:
            dqa[h] += dq
        elif level == 3:
            dqa[h] = placed(dq, level, h, 0.0)
        else:
            dqa[h] += placed(dq, level, h, 0.0)
        scaled_t = dot_t(eye[:DH, :DH], scaled).astype(BF)
        dv_t = dot(scaled_t, e)
        dk_t = dot(qts[level][h], ds) * SCALE
        both = jnp.transpose(jnp.concatenate([dk_t, dv_t], axis=0))
        if level == 0:
            dk0[h] = both[:, :DH]
            dv0[h] = both[:, DH:]
        else:
            shape = snd[level].shape[:-1] + (DH,)
            snd[level][..., grad_cols(h, 0)] = both[:, :DH].astype(BF).reshape(shape)
            snd[level][..., grad_cols(h, 1)] = both[:, DH:].astype(BF).reshape(shape)

    zb = z % 2

    def pair(level, hp):
        backward(level, 2 * hp)
        backward(level, 2 * hp + 1)

    def owed_core(level, hp):
        cols = slice(hp * 512, hp * 512 + 512)
        if level == 3:
            send(snd3.at[:, 1 - core, :, cols], cr3.at[:, :, cols], "c3_%d" % hp, to_seq(1))
        elif level == 2:
            send(snd2.at[:, 1 - core, :, cols], cr2.at[:, :, cols], "c2_%d" % hp, to_seq(1))
        else:
            send(snd1.at[1 - core, :, cols], cr1.at[:, cols], "c1_%d" % hp, to_seq(1))

    def owed_z(level, hp):
        cols = slice(hp * 512, hp * 512 + 512)
        if level == 3:
            arrived(cr3.at[:, :, cols], "c3_%d" % hp)
            for m in (2, 1, 3):
                zs3[m - 1, :, cols] = (snd3[z ^ m, core, :, cols].astype(F32) + cr3[z ^ m, :, cols].astype(F32)).astype(BF)
                send(zs3.at[m - 1, :, cols], rz3.at[m - 1, :, cols], "b3_%d_%d" % (m, hp), to_seq(2 * m))
        else:
            arrived(cr2.at[:, :, cols], "c2_%d" % hp)
            zs2[:, cols] = (snd2[zb ^ 1, core, :, cols].astype(F32) + cr2[zb ^ 1, :, cols].astype(F32)).astype(BF)
            send(zs2.at[:, cols], rz2.at[:, cols], "b2_1_%d" % hp, to_seq(2))

    result_second()
    grad_total(0)
    pair(3, 0)
    owed_core(3, 0)
    weight_third(1)
    pair(2, 0)
    owed_core(2, 0)
    owed_z(3, 0)
    pair(1, 0)
    owed_core(1, 0)
    owed_z(2, 0)
    pair(0, 0)
    weight_fourth(0)
    grad_total(1)
    pair(3, 1)
    owed_core(3, 1)
    pair(2, 1)
    owed_core(2, 1)
    owed_z(3, 1)
    pair(1, 1)
    owed_core(1, 1)
    owed_z(2, 1)
    weight_fourth(1)
    pair(0, 1)

    def natural(dst, hp):
        cols = slice(hp * 256, hp * 256 + 256)
        dst[:, cols] = dot(unperm[...], back[:, cols]).astype(BF)

    def key_total(hp):
        cols_in = slice(hp * 512, hp * 512 + 512)
        arrived(cr1.at[:, cols_in], "c1_%d" % hp)
        arrived(rz2.at[:, cols_in], "b2_1_%d" % hp)
        for m in (1, 3, 2):
            arrived(rz3.at[m - 1, :, cols_in], "b3_%d_%d" % (m, hp))
        for which, start_grad, dst in ((0, dk0, dk_o), (1, dv0, dv_o)):
            for h in (2 * hp, 2 * hp + 1):
                total = start_grad[h]
                cols = grad_cols(h, which)
                owed = snd1[core, :, cols].astype(F32) + cr1[:, cols].astype(F32)
                total += placed(owed, 1, h, 0.0)
                owed = snd2[zb, core, :, cols].astype(F32) + cr2[zb, :, cols].astype(F32) + rz2[:, cols].astype(F32)
                total += placed(owed, 2, h, 0.0)
                owed = snd3[z, core, :, cols].astype(F32) + cr3[z, :, cols].astype(F32)
                for m in range(3):
                    owed += rz3[m, :, cols].astype(F32)
                total += placed(owed, 3, h, 0.0)
                back[:, h * DH : (h + 1) * DH] = total.astype(BF)
            natural(dst, hp)

    key_total(0)
    for h in range(HL):
        back[:, h * DH : (h + 1) * DH] = dqa[h].astype(BF)
    natural(dq_o, 0)
    natural(dq_o, 1)
    written = [local(dq_o, dq_out, 5)]

    for rh, name in ((0, "r%da"), (1, "r%db")):
        arrived(res_r.at[0, rh * 256 : rh * 256 + 256], name % 1)
        arrived(res_r.at[1, rh * 256 : rh * 256 + 256], name % 3)

    def result_total(b):
        rows = pl.ds(pl.multiple_of(b * 128, 128), 128)
        res_o[rows, :] = (res_f[1, rows, :] + res_r[0, rows, :].astype(F32) + res_r[1, rows, :].astype(F32)).astype(BF)

    loop(4, result_total)
    written.append(local(res_o, res_out, 6))
    key_total(1)
    written.append(local(dk_o, dk_out, 7))
    written.append(local(dv_o, dv_out, 8))

    for source in range(2):

        @pl.when(jnp.logical_not((yh == source) & (q == yh)))
        def _(source=source):
            arrived(gy_r.at[source], "y%d" % source)

    gw_o[...] = (gy_r[0].astype(F32) + gy_r[1].astype(F32)).astype(BF)
    written.append(local(gw_o, gw_out, 9))

    last_hop(1).wait_send()

    @pl.when(yh != q)
    def _():
        last_hop(0).wait_send()

    for copy in sent.values():
        copy.wait_send()
    for copy in written:
        copy.wait()


def hand_over(*refs):
    sources, targets, held, sems = refs[:5], refs[5:10], refs[10:15], refs[15]
    reads = [pltpu.make_async_copy(sources[i], held[i], sems.at[0, i]) for i in range(5)]
    writes = [pltpu.make_async_copy(held[i], targets[i], sems.at[1, i]) for i in range(5)]
    for copy in reads:
        copy.start()
    for i in range(5):
        reads[i].wait()
        writes[i].start()
    for copy in writes:
        copy.wait()


def shards(queries, keys, values, offsets, out_weight, out_grad):
    wide = jax.ShapeDtypeStruct((R, C), BF)
    any_spec = pl.BlockSpec(memory_space=pl.ANY)

    def bf(*shape):
        return pltpu.VMEM(shape, BF)

    def f32(*shape):
        return pltpu.VMEM(shape, F32)

    count = len(NAMES)
    outs = (wide, wide, wide, wide, jax.ShapeDtypeStruct((512, 256), BF))
    made = pl.pallas_call(
        kernel,
        out_shape=outs,
        in_specs=[pl.BlockSpec(memory_space=pltpu.SMEM)] + [any_spec] * 5,
        out_specs=[any_spec] * 5,
        scratch_shapes=[
            bf(R, C), bf(R, C), bf(R, C), bf(R, C), bf(512, 256),
            bf(3, R, C), bf(R, R), bf(R, R), bf(R, R),
            bf(HL, R, DH), bf(HL, R, DH), bf(HL, R, DH),
            bf(2, 256, 1024), bf(4, 128, 1024), bf(8, 64, 1024),
            bf(HL, 512, R), bf(HL, 256, R), bf(HL, 128, R), bf(HL, 64, R),
            f32(HL, 512, DH), f32(HL, 256, DH), f32(HL, 128, DH), f32(HL, 64, DH),
            f32(HL, R, DH), f32(HL, R, DH), f32(HL, R, DH),
            bf(HL, R, DH), bf(2, R, C), bf(2, C, R),
            bf(4, R, C), bf(2, C, 2048),
            f32(2, R, 256), bf(2, R, 256), bf(2, R, 256), bf(HL, R, DH),
            bf(3, R, C), bf(256, C), bf(256, C), bf(2, R, C), f32(2, R, C),
            bf(2, 4, C, 256), bf(2, 4, C, 256),
            bf(2, 3, C, 256), bf(2, 256, 256), bf(2, 256, 256), bf(2, 2, C, 256), f32(2, 2, 256, 256), f32(2, C, 256),
            bf(2, 512, 256), bf(2, 512, 256),
            f32(HL, R, DH), f32(HL, R, DH), f32(HL, R, DH),
            bf(2, 256, 1024), bf(2, 2, 128, 1024), bf(4, 2, 64, 1024),
            bf(256, 1024), bf(2, 128, 1024), bf(4, 64, 1024),
            bf(128, 1024), bf(3, 64, 1024), bf(128, 1024), bf(3, 64, 1024),
            bf(R, C),
            bf(HL, DH, 512), bf(HL, DH, 256), bf(HL, DH, 128), bf(HL, DH, 64),
            pltpu.SemaphoreType.DMA((count,)), pltpu.SemaphoreType.DMA((count,)), pltpu.SemaphoreType.DMA((12,)),
        ],
        compiler_params=pltpu.CompilerParams(
            collective_id=0, has_side_effects=True, vmem_limit_bytes=60 * 1024 * 1024
        ),
    )(offsets, queries, keys, values, out_weight, out_grad)
    return pl.pallas_call(
        hand_over, out_shape=outs, in_specs=[any_spec] * 5, out_specs=[any_spec] * 5,
        scratch_shapes=[pltpu.VMEM(out.shape, BF) for out in outs] + [pltpu.SemaphoreType.DMA((2, 5))],
        compiler_params=pltpu.CompilerParams(vmem_limit_bytes=60 * 1024 * 1024),
    )(*made)


def solution(mesh):
    return jax.shard_map(
        shards,
        mesh=mesh,
        in_specs=(
            P("seq", "tp"),
            P("seq", "tp"),
            P("seq", "tp"),
            P(),
            P("tp", None),
            P("seq", "tp"),
        ),
        out_specs=(P("seq", "tp"), P("seq", "tp"), P("seq", "tp"), P("seq", "tp"), P("tp", "seq")),
        check_vma=False,
    )
```
